128 devices in a mesh: branch: 2 (over y_hi), res: 64 (over y_lo, z, x, core).
Axes of the slice: x: 4, y: 4 (y_hi: 2, y_lo: 2; y = y_hi * 2 + y_lo), z: 4, core: 2. Of those that a mesh axis runs over, the one named last changes fastest.
Arguments:
- homolog_activations: bfloat16 [64, 1024, 256], P(None, ('branch', 'res')), may hold values from -6 to 6
- standardize_multiplier: float32 [256], replicated, may hold values from 0.5 to 1.5
- first_factor_matrix: bfloat16 [256, 32], replicated, may hold values from -0.375 to 0.375
- second_factor_matrix: bfloat16 [256, 32], replicated, may hold values from -0.375 to 0.375
- final_matrix: bfloat16 [1024, 128], replicated, may hold values from -1.5 to 1.5
- final_offset: float32 [128], replicated, may hold values from -3 to 3
- same_molecule_offset: float32 [128], replicated, may hold values from -3 to 3
- edge_activations: bfloat16 [1024, 1024, 128], P(('branch', 'res')), may hold values from -6 to 6
- edge_result_sensitivity: bfloat16 [1024, 1024, 128], P(('branch', 'res')), may hold values from -24 to 24
- padding_indicator: int32 [1024], P(('branch', 'res')), may hold values from 0 to 1, as said below
- molecule_identity: int32 [1024], P(('branch', 'res')), may hold values from 0 to 63, as said below
Outputs:
- updated_pair_state: bfloat16 [1024, 1024, 128], P(('branch', 'res'))
- alignment_gradient: float32 [64, 1024, 256], P(None, ('branch', 'res'))
The draws below stay inside these ranges and needn't reach their ends.
Inputs may be any that keep to these rules, and one draw needn't show every extreme that they name: `padding_indicator`: 1 on the first 512 residues; each of the last 512 residues has its own value, 0 or 1, and the last residue is 0. `molecule_identity`: never falls along the residues; each chain is a run of residues.
All inputs are finite; a program needn't handle non-finite values.
Results may differ from the reference program's by a relative error of at most 0.0064.
Values may be sent and summed in bfloat16 or wider, within the bound.
A program may use at most 192 MiB of HBM per device.

```python
import jax
import jax.numpy as jnp
from jax import lax

HOMOLOG_COUNT = 64
SEQUENCE_FEATURE = 256
FACTOR_WIDTH = 32
EDGE_FEATURES = 128
SEQUENCE_LENGTH = 1024


def draw_padding_indicator(key, part):
    key = jax.random.fold_in(key, 11)
    places = jnp.arange(SEQUENCE_LENGTH, dtype=jnp.int32)
    tail_start = SEQUENCE_LENGTH - SEQUENCE_LENGTH // 2
    coins = jax.random.randint(key, (SEQUENCE_LENGTH,), 0, 2).astype(jnp.int32)
    mask = jnp.where(places < tail_start, 1, coins).astype(jnp.int32)
    mask = jnp.where(places == SEQUENCE_LENGTH - 1, 0, mask).astype(jnp.int32)
    return mask


def draw_molecule_identity(key, part):
    key = jax.random.fold_in(key, 12)
    chains = SEQUENCE_LENGTH // 16
    order = jax.random.permutation(key, SEQUENCE_LENGTH - 1).astype(jnp.int32) + 1
    picked = order[:chains - 1]
    starts = jnp.zeros((SEQUENCE_LENGTH,), jnp.int32).at[picked].set(1)
    return jnp.cumsum(starts).astype(jnp.int32)


def spiked(drawn, rng, source, target, parts, factor):
    def block_of(axis_at):
        return (jnp.arange(drawn.shape[axis_at]) // (drawn.shape[axis_at] // parts)).reshape((-1,) + (1,) * (drawn.ndim - 1 - axis_at))

    first = jax.random.permutation(rng, parts)[block_of(target)]
    other_side = (block_of(target) + parts // 2) % parts
    return jnp.where((block_of(source) == first) | (block_of(source) == other_side), factor * drawn, drawn)


def block_scale(stream_key, shape, cuts, least, high):
    factor_of, own = 1.0, jax.random.fold_in(stream_key, 6)
    for position, shards_of in cuts:
        heights = jnp.exp(jax.random.uniform(jax.random.fold_in(own, position), (shards_of,), jnp.float32, least / len(cuts), high / len(cuts)))
        factor_of = factor_of * jnp.repeat(heights, shape[position] // shards_of).reshape([-1 if axis == position else 1 for axis in range(len(shape))])
    return factor_of


def bell_draw(key, dims, spread, limit, shards=(), kind=jnp.bfloat16):
    entries = spread * jax.random.normal(key, dims, jnp.float32)
    if shards:
        entries = entries * block_scale(key, dims, shards, -0.22, 0.18)
    return jnp.clip(entries, -limit, limit).astype(kind)


def gaussian_with(stream_key, extent, scale, reach, split, heavy, kind=jnp.bfloat16):
    values = scale * jax.random.normal(stream_key, extent, jnp.float32)
    if split:
        values = values * block_scale(stream_key, extent, split, -0.22, 0.18)
    return jnp.clip(spiked(values, jax.random.fold_in(stream_key, 3), *heavy), -reach, reach).astype(kind)


def setup_inputs(seed: int = 0) -> dict:
    streams_of = jax.random.split(jax.random.key(seed), 12)
    homolog_activations = bell_draw(streams_of[0], (HOMOLOG_COUNT, SEQUENCE_LENGTH, SEQUENCE_FEATURE), 1.0, 6.0, ((1, 128),))
    standardize_multiplier = jnp.clip(1.0 + 0.1 * jax.random.normal(streams_of[1], (SEQUENCE_FEATURE,), jnp.float32), 0.5, 1.5)
    first_factor_matrix = bell_draw(streams_of[2], (SEQUENCE_FEATURE, FACTOR_WIDTH), SEQUENCE_FEATURE ** -0.5, 0.375)
    second_factor_matrix = bell_draw(streams_of[3], (SEQUENCE_FEATURE, FACTOR_WIDTH), SEQUENCE_FEATURE ** -0.5, 0.375)
    final_matrix = bell_draw(streams_of[4], (FACTOR_WIDTH * FACTOR_WIDTH, EDGE_FEATURES), (FACTOR_WIDTH * FACTOR_WIDTH // HOMOLOG_COUNT) ** -0.5, 1.5)
    final_offset = bell_draw(streams_of[5], (EDGE_FEATURES,), 0.5, 3.0, (), jnp.float32)
    same_molecule_offset = bell_draw(streams_of[6], (EDGE_FEATURES,), 0.5, 3.0, (), jnp.float32)
    edge_activations = bell_draw(streams_of[7], (SEQUENCE_LENGTH, SEQUENCE_LENGTH, EDGE_FEATURES), 1.0, 6.0, ((0, 128),))
    edge_result_sensitivity = gaussian_with(streams_of[8], (SEQUENCE_LENGTH, SEQUENCE_LENGTH, EDGE_FEATURES), 1.0, 24.0, ((0, 128),), (0, 1, 128, 5.5))
    padding_indicator = draw_padding_indicator(jax.random.fold_in(streams_of[11], 71), 0)
    molecule_identity = draw_molecule_identity(jax.random.fold_in(streams_of[11], 71), 0)
    return {"homolog_activations": homolog_activations, "standardize_multiplier": standardize_multiplier, "first_factor_matrix": first_factor_matrix, "second_factor_matrix": second_factor_matrix, "final_matrix": final_matrix, "final_offset": final_offset, "same_molecule_offset": same_molecule_offset, "edge_activations": edge_activations, "edge_result_sensitivity": edge_result_sensitivity, "padding_indicator": padding_indicator, "molecule_identity": molecule_identity}


EPSILON = 1e-05

def moment_summary(homolog_activations, standardize_multiplier):
    contribution_sequences = homolog_activations.astype(jnp.float32)
    centred = contribution_sequences - lax.optimization_barrier(jnp.mean(contribution_sequences, axis=-1, keepdims=True))
    averaged_result = lax.rsqrt(lax.optimization_barrier(jnp.mean(centred * centred, axis=-1, keepdims=True)) + EPSILON)
    whitened_features = centred * averaged_result
    return (whitened_features, averaged_result, (whitened_features * standardize_multiplier).astype(jnp.bfloat16))

def reference(homolog_activations, standardize_multiplier, first_factor_matrix, second_factor_matrix, final_matrix, final_offset, same_molecule_offset, edge_activations, edge_result_sensitivity, padding_indicator, molecule_identity):
    whitened_features, averaged_result, standardized_features = moment_summary(homolog_activations, standardize_multiplier)
    first_factor = jnp.dot(standardized_features, first_factor_matrix, preferred_element_type=jnp.float32).astype(jnp.bfloat16)
    right = jnp.dot(standardized_features, second_factor_matrix, preferred_element_type=jnp.float32).astype(jnp.bfloat16)
    keep = padding_indicator.astype(jnp.float32)
    left_wide = first_factor.astype(jnp.float32)
    second_factor_flat = right.astype(jnp.float32)
    block = 8
    count = SEQUENCE_LENGTH // block

    def step(running_total, index):
        start = index.astype(jnp.int32) * block
        first_factor_sequences = lax.dynamic_slice_in_dim(left_wide, start, block, 1)
        pair_rows = lax.dynamic_slice_in_dim(edge_activations, start, block, 0)
        cot_rows = lax.dynamic_slice_in_dim(edge_result_sensitivity, start, block, 0)
        keep_rows = lax.dynamic_slice_in_dim(keep, start, block, 0)
        chain_rows = lax.dynamic_slice_in_dim(molecule_identity, start, block, 0)
        tensor_product = (jnp.einsum('uvp,ufz->vfpz', first_factor_sequences, second_factor_flat) / HOMOLOG_COUNT).astype(jnp.bfloat16)
        project = jnp.dot(tensor_product.reshape(block * SEQUENCE_LENGTH, FACTOR_WIDTH * FACTOR_WIDTH), final_matrix, preferred_element_type=jnp.float32).reshape(block, SEQUENCE_LENGTH, EDGE_FEATURES)
        weight_mask = keep_rows[:, None] * keep[None, :]
        same = (chain_rows[:, None] == molecule_identity[None, :]).astype(jnp.float32)
        update = weight_mask[:, :, None] * (project + final_offset + same[:, :, None] * same_molecule_offset)
        new_rows = (pair_rows.astype(jnp.float32) + update).astype(jnp.bfloat16)
        reverse_sweep = jnp.dot(cot_rows.reshape(block * SEQUENCE_LENGTH, EDGE_FEATURES), final_matrix.T, preferred_element_type=jnp.float32).reshape(block, SEQUENCE_LENGTH, FACTOR_WIDTH, FACTOR_WIDTH)
        reverse_sweep = lax.optimization_barrier((reverse_sweep * weight_mask[:, :, None, None]).astype(jnp.bfloat16)).astype(jnp.float32)
        sensitivity_sequences = jnp.einsum('prut,ort->opu', reverse_sweep, second_factor_flat) / HOMOLOG_COUNT
        running_total = running_total + jnp.einsum('fctr,nft->ncr', reverse_sweep, first_factor_sequences) / HOMOLOG_COUNT
        return (running_total, (new_rows, sensitivity_sequences))
    empty_accumulator = jnp.zeros((HOMOLOG_COUNT, SEQUENCE_LENGTH, FACTOR_WIDTH), jnp.float32)
    grad_right, (new_blocks, sensitivity_tiles) = lax.scan(step, empty_accumulator, jnp.arange(count))
    updated_pair_state = new_blocks.reshape(SEQUENCE_LENGTH, SEQUENCE_LENGTH, EDGE_FEATURES)
    sensitivity_first_factor = jnp.transpose(sensitivity_tiles, (1, 0, 2, 3)).reshape(HOMOLOG_COUNT, SEQUENCE_LENGTH, FACTOR_WIDTH)
    grad_normed = jnp.dot(sensitivity_first_factor.astype(jnp.bfloat16), first_factor_matrix.T, preferred_element_type=jnp.float32)
    grad_normed = grad_normed + jnp.dot(grad_right.astype(jnp.bfloat16), second_factor_matrix.T, preferred_element_type=jnp.float32)
    gain_applied = grad_normed * standardize_multiplier
    alignment_gradient = averaged_result * (gain_applied - lax.optimization_barrier(jnp.mean(gain_applied, axis=-1, keepdims=True)) - whitened_features * lax.optimization_barrier(jnp.mean(gain_applied * whitened_features, axis=-1, keepdims=True)))
    return (updated_pair_state, alignment_gradient)
```

```python
import jax
import jax.numpy as jnp
from jax import lax
from jax.experimental import pallas as pl
from jax.experimental.pallas import tpu as pltpu
from jax.sharding import PartitionSpec as P

MESH = pl.DeviceIdType.MESH
F32 = jnp.float32
BF16 = jnp.bfloat16

SEQS = 64
FEAT = 256
FACTOR = 32
EDGE = 128
LENGTH = 1024
OWN = 8
HALF = 1024
WIDE = HALF + 128
EPSILON = 1e-05

PARTS = (0, 1, 2)
GATHER_LANES = ((0, 384), (384, 384), (768, 384))
SCATTER_LANES = ((0, 384), (384, 384), (768, 256))


def axes_of(part):
    return (part % 3, (part + 1) % 3, (part + 2) % 3)


def nt(a, b):
    return lax.dot_general(a, b, (((1,), (1,)), ((), ())), preferred_element_type=F32)


def kernel(
    x_ref, gain_ref, w1_ref, w2_ref, wf_ref, off_ref, smo_ref, edge_hbm, cot_hbm, pad_ref, mol_ref,
    out_hbm, grad_ref,
    cot, edge, right, proj, terms, peer_out, peer_in, slab1, sum1, slab2, sum2, slab3,
    gmat, unit_s, rstd_s, wff, wflat, left_s, grad_s, blk_out, blk_in, fin_s, fin_out, fin_in,
    load_sem, store_sem,
    ag_send, ag_recv, fw_send, fw_recv, rs_send, rs_recv, pr_send, pr_recv, misc_send, misc_recv,
):
    branch, res = lax.axis_index("branch"), lax.axis_index("res")
    core = res % 2
    me = (branch * 2 + res // 32, (res // 8) % 4, (res // 2) % 4)

    def device(at, c):
        return (at[0] // 2, (at[0] % 2) * 32 + at[1] * 8 + at[2] * 2 + c)

    def shifted(axis, k):
        at = list(me)
        at[axis] = (at[axis] + k) % 4
        return at

    sibling = device(me, 1 - core)

    barrier = pltpu.get_barrier_semaphore()
    for axis in range(3):
        for k in (1, 2, 3):
            pl.semaphore_signal(barrier, inc=1, device_id=device(shifted(axis, k), core), device_id_type=MESH)
    pl.semaphore_signal(barrier, inc=1, device_id=sibling, device_id_type=MESH)

    cot_loads = [
        pltpu.make_async_copy(cot_hbm.at[i], cot.at[:, pl.ds(i * EDGE, EDGE)], load_sem.at[i])
        for i in range(OWN)
    ]
    for cp in cot_loads:
        cp.start()
    edge_load = pltpu.make_async_copy(edge_hbm, edge, load_sem.at[OWN])
    edge_load.start()

    xs = x_ref[...].astype(F32).reshape(SEQS * OWN, FEAT)
    centred = xs - jnp.mean(xs, axis=-1, keepdims=True)
    rstd = lax.rsqrt(jnp.mean(centred * centred, axis=-1, keepdims=True) + EPSILON)
    unit = centred * rstd
    unit_s[...] = unit
    rstd_s[...] = jnp.broadcast_to(rstd, (SEQS * OWN, 128))
    normed = (unit * gain_ref[...]).astype(BF16)

    lane = lax.broadcasted_iota(jnp.int32, (FACTOR, FEAT), 1)
    row = lax.broadcasted_iota(jnp.int32, (FACTOR, FEAT), 0)
    spread = jnp.where(lane // 8 == row, 1.0, 0.0).astype(BF16)
    w2e = jnp.dot(w2_ref[...], spread, preferred_element_type=F32).astype(BF16)

    rows8 = lax.broadcasted_iota(jnp.int32, (OWN, 128), 0)
    keep_col = jnp.zeros((OWN, 128), F32)
    mol_col = jnp.zeros((OWN, 128), F32)
    for i in range(OWN):
        keep_col = jnp.where(rows8 == i, pad_ref[i].astype(F32), keep_col)
        mol_col = jnp.where(rows8 == i, mol_ref[i].astype(F32), mol_col)
    keep_one = keep_col[:, :1]

    lane4 = lax.broadcasted_iota(jnp.int32, (8, OWN, FEAT), 2) % 8
    slot4 = lax.broadcasted_iota(jnp.int32, (8, OWN, FEAT), 0)
    mine = lane4 == slot4
    right_e = jnp.dot(normed, w2e, preferred_element_type=F32).astype(BF16).astype(F32)
    right_e = right_e.reshape(8, 8, OWN, FEAT)
    flat = [
        jnp.sum(jnp.where(mine, right_e[h], 0.0), axis=0) * keep_one for h in range(8)
    ]
    half0 = jnp.concatenate(flat[:4] + [keep_col], axis=1)
    half1 = jnp.concatenate(flat[4:] + [mol_col], axis=1)
    first = core == 0
    blk_out[...] = jnp.where(first, half1, half0)
    own_blk = jnp.where(first, half0, half1)

    pl.semaphore_wait(barrier, 10)
    blk_copy = pltpu.make_async_remote_copy(
        blk_out, blk_in, misc_send.at[0], misc_recv.at[0], device_id=sibling, device_id_type=MESH
    )
    blk_copy.start()

    left_s[...] = jnp.dot(normed, w1_ref[...], preferred_element_type=F32).astype(BF16).astype(F32)
    wff[...] = wf_ref[...].astype(F32)
    for b in range(FACTOR):
        wflat[:, b * EDGE : (b + 1) * EDGE] = wff[pl.ds(b, FACTOR, stride=FACTOR), :].astype(BF16)
    left = jnp.concatenate(
        [
            left_s[pl.ds(i, SEQS, stride=OWN), :] * (pad_ref[i].astype(F32) * (1.0 / SEQS))
            for i in range(OWN)
        ],
        axis=0,
    ).astype(BF16)

    def gather_ref(half, part, phase, at):
        idx = list(at)
        for axis in axes_of(part)[:phase]:
            idx[axis] = slice(None)
        lo, width = GATHER_LANES[part]
        return right.at[half, idx[0], idx[1], idx[2], :, pl.ds(lo, width)]

    def gather_send(part, phase, k):
        block = gather_ref(core, part, phase, me)
        return pltpu.make_async_remote_copy(
            block, block, ag_send.at[part, phase, k - 1], ag_recv.at[part, phase, k - 1],
            device_id=device(shifted(axes_of(part)[phase], k), core), device_id_type=MESH,
        )

    def gather_recv(part, phase, k):
        block = gather_ref(core, part, phase, shifted(axes_of(part)[phase], 4 - k))
        return pltpu.make_async_remote_copy(
            block, block, ag_send.at[part, phase, k - 1], ag_recv.at[part, phase, k - 1],
            device_id=device(shifted(axes_of(part)[phase], 4 - k), core), device_id_type=MESH,
        )

    def forward(part, k, half):
        block = gather_ref(half, part, 2, shifted(axes_of(part)[2], (4 - k) % 4))
        return pltpu.make_async_remote_copy(
            block, block, fw_send.at[part, k], fw_recv.at[part, k],
            device_id=sibling, device_id_type=MESH,
        )

    def scatter_copy(part, phase, k):
        axes = axes_of(part)
        lo, width = SCATTER_LANES[part]
        lanes = pl.ds(lo, width)
        to = shifted(axes[phase], k)
        there = to[axes[phase]]
        if phase == 0:
            idx = [slice(None)] * 3
            idx[axes[0]] = there
            src = terms.at[idx[0], idx[1], idx[2], :, lanes]
            dst = slab1.at[k - 1, :, :, :, lanes]
        elif phase == 1:
            idx = [slice(None)] * 2
            idx[0 if axes[1] < axes[2] else 1] = there
            src = sum1.at[idx[0], idx[1], :, lanes]
            dst = slab2.at[k - 1, :, :, lanes]
        else:
            src = sum2.at[there, :, lanes]
            dst = slab3.at[k - 1, :, lanes]
        return pltpu.make_async_remote_copy(
            src, dst, rs_send.at[part, phase, k - 1], rs_recv.at[part, phase, k - 1],
            device_id=device(to, core), device_id_type=MESH,
        )

    def scatter_add(part, phase):
        axes = axes_of(part)
        lo, width = SCATTER_LANES[part]
        lanes = pl.ds(lo, width)
        for k in (1, 2, 3):
            scatter_copy(part, phase, k).wait_recv()
        here = me[axes[phase]]
        if phase == 0:
            idx = [slice(None)] * 3
            idx[axes[0]] = here
            total = terms[idx[0], idx[1], idx[2], :, lanes].astype(F32)
            for k in range(3):
                total += slab1[k, :, :, :, lanes].astype(F32)
            sum1[:, :, :, lanes] = total.astype(BF16)
        elif phase == 1:
            idx = [slice(None)] * 2
            idx[0 if axes[1] < axes[2] else 1] = here
            total = sum1[idx[0], idx[1], :, lanes].astype(F32)
            for k in range(3):
                total += slab2[k, :, :, lanes].astype(F32)
            sum2[:, :, lanes] = total.astype(BF16)
        else:
            total = sum2[here, :, lanes].astype(F32)
            for k in range(3):
                total += slab3[k, :, lanes].astype(F32)
            fin_s[:, lanes] = total

    def start_all(make, phase):
        for part in PARTS:
            for k in (1, 2, 3):
                make(part, phase, k).start()

    blk_copy.wait_recv()
    theirs = blk_in[...]
    block16 = jnp.concatenate(
        [jnp.where(first, own_blk, theirs), jnp.where(first, theirs, own_blk)], axis=0
    ).astype(BF16)
    right[core, me[0], me[1], me[2]] = block16
    start_all(gather_send, 0)

    def proj_step(n, carry):
        y = jnp.dot(left, wflat[:, pl.ds(pl.multiple_of(n * 256, 256), 256)], preferred_element_type=F32)
        for i in range(OWN):
            for h in range(8):
                tile = y[i * SEQS + h * 8 : i * SEQS + h * 8 + 8]
                pair = jnp.concatenate([tile[:, :EDGE], tile[:, EDGE:]], axis=0).astype(BF16)
                proj[pl.ds(pl.multiple_of(h * 256 + n * 16, 16), 16), i * EDGE : (i + 1) * EDGE] = pair
        return carry

    lax.fori_loop(0, 16, proj_step, 0)

    for cp in cot_loads:
        cp.wait()

    for part in PARTS:
        for k in (1, 2, 3):
            gather_recv(part, 0, k).wait_recv()
    start_all(gather_send, 1)

    def peer_copy(q):
        return pltpu.make_async_remote_copy(
            peer_out.at[q], peer_in.at[q], pr_send.at[q], pr_recv.at[q],
            device_id=sibling, device_id_type=MESH,
        )

    def half_terms(q, half):
        rows = cot[pl.ds(pl.multiple_of(q * 256, 256), 256), :]
        return nt(rows, proj[pl.ds(pl.multiple_of(half * HALF, HALF), HALF), :])

    def peer_step(q, carry):
        peer_out[q] = half_terms(q, 1 - core).astype(BF16)
        peer_copy(q).start()
        return carry

    lax.fori_loop(0, 4, peer_step, 0)

    for part in PARTS:
        for k in (1, 2, 3):
            gather_recv(part, 1, k).wait_recv()
    start_all(gather_send, 2)
    for part in PARTS:
        forward(part, 0, core).start()

    def own_step(q, carry):
        total = half_terms(q, core)
        peer_copy(q).wait_recv()
        total = total + peer_in[q].astype(F32)
        terms[q] = total.astype(BF16).reshape(4, 4, 16, HALF)
        return carry

    lax.fori_loop(0, 4, own_step, 0)
    start_all(scatter_copy, 0)

    for k in (1, 2, 3):
        for part in PARTS:
            gather_recv(part, 2, k).wait_recv()
            forward(part, k, core).start()
    for k in (0, 1, 2, 3):
        for part in PARTS:
            forward(part, k, 1 - core).wait_recv()

    edge_load.wait()

    def store(q):
        rows = pl.ds(pl.multiple_of(q * 256, 256), 256)
        return pltpu.make_async_copy(edge.at[:, rows, :], out_hbm.at[:, rows, :], store_sem.at[q])

    def pair_step(q, carry):
        r0 = right[0, q, :, :, :, 0:HALF].reshape(256, HALF)
        r1 = right[1, q, :, :, :, 0:HALF].reshape(256, HALF)
        keep_j = right[0, q, :, :, :, HALF:WIDE].reshape(256, 128).astype(F32)
        mol_j = right[1, q, :, :, :, HALF:WIDE].reshape(256, 128).astype(F32)
        u = jnp.dot(r0, proj[:HALF, :], preferred_element_type=F32)
        u += jnp.dot(r1, proj[HALF:, :], preferred_element_type=F32)
        rows = pl.ds(pl.multiple_of(q * 256, 256), 256)
        for i in range(OWN):
            same = jnp.where(mol_j == mol_ref[i].astype(F32), 1.0, 0.0)
            extra = (keep_j * pad_ref[i].astype(F32)) * (off_ref[...] + same * smo_ref[...])
            upd = u[:, i * EDGE : (i + 1) * EDGE] + extra
            edge[i, rows, :] = (edge[i, rows, :].astype(F32) + upd).astype(BF16)
        store(q).start()
        return carry

    lax.fori_loop(0, 2, pair_step, 0)
    for part in PARTS:
        scatter_add(part, 0)
        for k in (1, 2, 3):
            scatter_copy(part, 1, k).start()
    lax.fori_loop(2, 4, pair_step, 0)
    for part in PARTS:
        scatter_add(part, 1)
        for k in (1, 2, 3):
            scatter_copy(part, 2, k).start()

    def left_step(h, carry):
        half = h // 4
        lo = pl.multiple_of((h % 4) * 256, 256)
        r = right[half, :, :, :, :, pl.ds(lo, 256)].reshape(LENGTH, 256)
        g = lax.dot_general(r, cot[...], (((0,), (0,)), ((), ())), preferred_element_type=F32)
        for b in range(FACTOR):
            tile = g[b * 8 : b * 8 + 8]
            for i in range(0, OWN, 2):
                pair = jnp.concatenate(
                    [tile[:, i * EDGE : (i + 1) * EDGE], tile[:, (i + 1) * EDGE : (i + 2) * EDGE]], axis=0
                ).astype(BF16)
                gmat[pl.ds(pl.multiple_of(h * 64 + i * 8, 16), 16), b * EDGE : (b + 1) * EDGE] = pair
        return carry

    lax.fori_loop(0, 8, left_step, 0)

    for part in PARTS:
        scatter_add(part, 2)
    fin = fin_s[...]
    fin_out[...] = jnp.where(first, fin[8:], fin[:8])
    fin_mine = jnp.where(first, fin[:8], fin[8:])
    fin_copy = pltpu.make_async_remote_copy(
        fin_out, fin_in, misc_send.at[1], misc_recv.at[1], device_id=sibling, device_id_type=MESH
    )
    fin_copy.start()

    gl = nt(gmat[...], wflat[...])
    for h in range(8):
        for i in range(OWN):
            tile = gl[h * 64 + i * 8 : h * 64 + i * 8 + 8] * (pad_ref[i].astype(F32) * (1.0 / SEQS))
            grad_s[pl.ds(h * 64 + i, 8, stride=OWN), :] = tile
    grad_normed = nt(grad_s[...].astype(BF16), w1_ref[...])

    fin_copy.wait_recv()
    fin_theirs = fin_in[...]
    lo_half = jnp.where(first, fin_mine, fin_theirs) * keep_one
    hi_half = jnp.where(first, fin_theirs, fin_mine) * keep_one
    spread_rows = []
    for h in range(8):
        src = lo_half if h < 4 else hi_half
        base = src[:, (h % 4) * 256 : (h % 4) * 256 + 256]
        spread_rows.append(jnp.where(mine, base[None], 0.0).reshape(8 * OWN, FEAT))
    gr = jnp.concatenate(spread_rows, axis=0).astype(BF16)
    grad_normed = grad_normed + nt(gr, w2e)

    gained = grad_normed * gain_ref[...]
    unit = unit_s[...]
    rstd = rstd_s[:, :1]
    grad = rstd * (
        gained
        - jnp.mean(gained, axis=-1, keepdims=True)
        - unit * jnp.mean(gained * unit, axis=-1, keepdims=True)
    )
    grad_ref[...] = grad.reshape(SEQS, OWN, FEAT)

    blk_copy.wait_send()
    fin_copy.wait_send()
    for part in PARTS:
        for phase in range(3):
            for k in (1, 2, 3):
                gather_send(part, phase, k).wait_send()
                scatter_copy(part, phase, k).wait_send()
        for k in range(4):
            forward(part, k, core).wait_send()
    for q in range(4):
        peer_copy(q).wait_send()
        store(q).wait()


def local(x, gain, w1, w2, wf, off, smo, edge, cot, pad, mol):
    vmem = pl.BlockSpec(memory_space=pltpu.VMEM)
    smem = pl.BlockSpec(memory_space=pltpu.SMEM)
    hbm = pl.BlockSpec(memory_space=pl.ANY)
    dma = pltpu.SemaphoreType.DMA
    return pl.pallas_call(
        kernel,
        out_shape=(
            jax.ShapeDtypeStruct(edge.shape, BF16),
            jax.ShapeDtypeStruct(x.shape, F32),
        ),
        in_specs=[vmem] * 7 + [hbm, hbm, smem, smem],
        out_specs=(hbm, vmem),
        scratch_shapes=[
            pltpu.VMEM((LENGTH, OWN * EDGE), BF16),
            pltpu.VMEM((OWN, LENGTH, EDGE), BF16),
            pltpu.VMEM((2, 4, 4, 4, 16, WIDE), BF16),
            pltpu.VMEM((2 * HALF, OWN * EDGE), BF16),
            pltpu.VMEM((4, 4, 4, 16, HALF), BF16),
            pltpu.VMEM((4, 256, HALF), BF16),
            pltpu.VMEM((4, 256, HALF), BF16),
            pltpu.VMEM((3, 4, 4, 16, HALF), BF16),
            pltpu.VMEM((4, 4, 16, HALF), BF16),
            pltpu.VMEM((3, 4, 16, HALF), BF16),
            pltpu.VMEM((4, 16, HALF), BF16),
            pltpu.VMEM((3, 16, HALF), BF16),
            pltpu.VMEM((SEQS * OWN, FACTOR * EDGE), BF16),
            pltpu.VMEM((SEQS * OWN, FEAT), F32),
            pltpu.VMEM((SEQS * OWN, 128), F32),
            pltpu.VMEM((FACTOR * FACTOR, EDGE), F32),
            pltpu.VMEM((FACTOR, FACTOR * EDGE), BF16),
            pltpu.VMEM((SEQS * OWN, FACTOR), F32),
            pltpu.VMEM((SEQS * OWN, FACTOR), F32),
            pltpu.VMEM((OWN, WIDE), F32),
            pltpu.VMEM((OWN, WIDE), F32),
            pltpu.VMEM((16, HALF), F32),
            pltpu.VMEM((OWN, HALF), F32),
            pltpu.VMEM((OWN, HALF), F32),
            dma((OWN + 1,)),
            dma((4,)),
            dma((3, 3, 3)),
            dma((3, 3, 3)),
            dma((3, 4)),
            dma((3, 4)),
            dma((3, 3, 3)),
            dma((3, 3, 3)),
            dma((4,)),
            dma((4,)),
            dma((2,)),
            dma((2,)),
        ],
        compiler_params=pltpu.CompilerParams(
            collective_id=0, has_side_effects=True, vmem_limit_bytes=56 * 2**20
        ),
        name="outer_product_mean",
    )(x, gain.reshape(1, FEAT), w1, w2, wf, off.reshape(1, EDGE), smo.reshape(1, EDGE), edge, cot, pad, mol)


def solution(mesh):
    rows = ("branch", "res")
    return jax.shard_map(
        local,
        mesh=mesh,
        in_specs=(
            P(None, rows, None), P(), P(), P(), P(), P(), P(),
            P(rows, None, None), P(rows, None, None), P(rows), P(rows),
        ),
        out_specs=(P(rows, None, None), P(None, rows, None)),
        check_vma=False,
    )
```

```python
import jax
import jax.numpy as jnp
from jax import lax
from jax.experimental import pallas as pl
from jax.experimental.pallas import tpu as pltpu
from jax.sharding import PartitionSpec as P

MESH = pl.DeviceIdType.MESH
F32 = jnp.float32
BF16 = jnp.bfloat16

SEQS = 64
FEAT = 256
FACTOR = 32
EDGE = 128
LENGTH = 1024
OWN = 8
HALF = 1024
GROUPS = HALF // 128
EPSILON = 1e-05

PARTS = (0, 1, 2)
STEPS = (1, 2, 3)


def axes_of(part):
    return (part % 3, (part + 1) % 3, (part + 2) % 3)


def sum_groups(part):
    return pl.ds(3 * part, 3 if part < 2 else GROUPS - 6)


def nt(a, b):
    return lax.dot_general(a, b, (((1,), (1,)), ((), ())), preferred_element_type=F32)


def normalise(x):
    xs = x.astype(F32).reshape(SEQS * OWN, FEAT)
    centred = xs - jnp.mean(xs, axis=-1, keepdims=True)
    rstd = lax.rsqrt(jnp.mean(centred * centred, axis=-1, keepdims=True) + EPSILON)
    return centred * rstd, rstd


def exchange_kernel(
    x_hbm, gain_hbm, w1t_hbm, w2t_hbm, wf_hbm, edge_hbm, cot_hbm, pad_hbm, mol_hbm,
    u_acc, labels, gn_ref, unit_ref, rstd_ref,
    x_ref, gain_ref, w1t_ref, w2t_ref, wf_ref, pad_ref, mol_ref,
    edge, cot, right, left_b, proj, terms, peer_out, peer_in, slab1, sum1, slab2, sum2, slab3,
    g_acc, gmat, wff, wflat, left_s, grad_s, blk_out, blk_in, fin_s, fin_out, fin_in,
    load_sem,
    ag_send, ag_recv, op_send, op_recv, fw_send, fw_recv,
    r0_send, r0_recv, rs_send, rs_recv, pr_send, pr_recv, misc_send, misc_recv,
):
    branch, res = lax.axis_index("branch"), lax.axis_index("res")
    core = res % 2
    first = core == 0
    me = (branch * 2 + res // 32, (res // 8) % 4, (res // 2) % 4)

    def device(at, c):
        return (at[0] // 2, (at[0] % 2) * 32 + at[1] * 8 + at[2] * 2 + c)

    def shifted(axis, k):
        at = list(me)
        at[axis] = (at[axis] + k) % 4
        return at

    def remote(src, dst, send, recv, to):
        return pltpu.make_async_remote_copy(src, dst, send, recv, device_id=to, device_id_type=MESH)

    sibling = device(me, 1 - core)

    small = (
        (x_hbm, x_ref), (gain_hbm, gain_ref), (w2t_hbm, w2t_ref), (w1t_hbm, w1t_ref),
        (wf_hbm, wf_ref), (pad_hbm, pad_ref), (mol_hbm, mol_ref),
    )
    small_loads = [
        pltpu.make_async_copy(src, dst, load_sem.at[OWN + n]) for n, (src, dst) in enumerate(small)
    ]
    for cp in small_loads:
        cp.start()

    barrier = pltpu.get_barrier_semaphore()
    for axis in range(3):
        for k in STEPS:
            pl.semaphore_signal(barrier, inc=1, device_id=device(shifted(axis, k), core), device_id_type=MESH)
    pl.semaphore_signal(barrier, inc=1, device_id=sibling, device_id_type=MESH)

    cot_loads = [
        pltpu.make_async_copy(cot_hbm.at[i], cot.at[:, :, :, :, pl.ds(i * EDGE, EDGE)], load_sem.at[i])
        for i in range(OWN)
    ]
    edge_load = pltpu.make_async_copy(edge_hbm, edge, load_sem.at[OWN + 7])
    for cp in cot_loads:
        cp.start()
    edge_load.start()

    for cp in small_loads:
        cp.wait()
    unit, rstd = normalise(x_ref[...])
    unit_ref[...] = unit
    rstd_ref[...] = jnp.broadcast_to(rstd, rstd_ref.shape)
    normed = (unit * gain_ref[...]).astype(BF16)

    lane = lax.broadcasted_iota(jnp.int32, (FACTOR, FEAT), 1)
    row = lax.broadcasted_iota(jnp.int32, (FACTOR, FEAT), 0)
    spread = jnp.where(lane // 8 == row, 1.0, 0.0).astype(BF16)
    w2e = lax.dot_general(
        spread, w2t_ref[...], (((0,), (0,)), ((), ())), preferred_element_type=F32
    ).astype(BF16)

    rows8 = lax.broadcasted_iota(jnp.int32, (OWN, 128), 0)
    keep_col = jnp.zeros((OWN, 128), F32)
    mol_col = jnp.zeros((OWN, 128), F32)
    for i in range(OWN):
        keep_col = jnp.where(rows8 == i, pad_ref[i].astype(F32), keep_col)
        mol_col = jnp.where(rows8 == i, mol_ref[i].astype(F32), mol_col)
    keep_one = keep_col[:, :1]

    lane4 = lax.broadcasted_iota(jnp.int32, (8, OWN, FEAT), 2) % 8
    slot4 = lax.broadcasted_iota(jnp.int32, (8, OWN, FEAT), 0)
    mine = lane4 == slot4
    right_e = nt(normed, w2e).astype(BF16).astype(F32).reshape(8, 8, OWN, FEAT)
    flat = [jnp.sum(jnp.where(mine, right_e[h], 0.0), axis=0) * keep_one for h in range(8)]
    half0 = jnp.concatenate(flat[:4] + [keep_col], axis=1)
    half1 = jnp.concatenate(flat[4:] + [mol_col], axis=1)
    blk_out[...] = jnp.where(first, half1, half0)
    own_blk = jnp.where(first, half0, half1)

    left_s[...] = nt(normed, w1t_ref[...]).astype(BF16).astype(F32)
    wff[...] = wf_ref[...].astype(F32)
    for b in range(FACTOR):
        wflat[:, b * EDGE : (b + 1) * EDGE] = wff[pl.ds(b, FACTOR, stride=FACTOR), :].astype(BF16)
    for i in range(OWN):
        rows = left_s[pl.ds(i, SEQS, stride=OWN), :] * (pad_ref[i].astype(F32) * (1.0 / SEQS))
        for half in range(2):
            left_b[half, i * 32 : i * 32 + 32, :] = rows[half * 32 : half * 32 + 32].astype(BF16)

    def proj_half(half):
        left = left_b[half]

        def step(m, carry):
            for v in range(4):
                n = m * 4 + v
                y = jnp.dot(left, wflat[:, pl.ds(pl.multiple_of(n * 256, 256), 256)], preferred_element_type=F32)
                for i in range(OWN):
                    for h in range(4):
                        tile = y[i * 32 + h * 8 : i * 32 + h * 8 + 8]
                        pair = jnp.concatenate([tile[:, :EDGE], tile[:, EDGE:]], axis=0).astype(BF16)
                        top = pl.multiple_of(half * HALF + h * 256 + n * 16, 16)
                        proj[pl.ds(top, 16), i * EDGE : (i + 1) * EDGE] = pair
            return carry

        lax.fori_loop(0, 4, step, 0)

    proj_half(1 - core)
    pl.semaphore_wait(barrier, 10)
    blk_copy = remote(blk_out, blk_in, misc_send.at[0], misc_recv.at[0], sibling)
    blk_copy.start()
    for cp in cot_loads:
        cp.wait()

    def plane_index(part, phase, at):
        idx = list(at)
        for axis in axes_of(part)[:phase]:
            idx[axis] = slice(None)
        return tuple(idx)

    def block_ref(half, part, phase, at):
        return right.at[(half, pl.ds(3 * part, 3)) + plane_index(part, phase, at)]

    def half_ref(half, part, at, upper):
        idx = list(plane_index(part, 2, at))
        idx[axes_of(part)[0]] = pl.ds(2 * upper, 2)
        return right.at[(half, pl.ds(3 * part, 3)) + tuple(idx)]

    def gather(part, phase, k, receive=False):
        axis = axes_of(part)[phase]
        at = shifted(axis, 4 - k) if receive else me
        block = block_ref(core, part, phase, at)
        to = device(shifted(axis, 4 - k if receive else k), core)
        return remote(block, block, ag_send.at[part, phase, k - 1], ag_recv.at[part, phase, k - 1], to)

    def opposite(part, upper, receive=False):
        axis = axes_of(part)[2]
        k = 3 if upper else 1
        at = shifted(axis, 2) if receive else shifted(axis, 4 - k)
        block = half_ref(core, part, at, upper)
        to = device(shifted(axis, 4 - k if receive else k), core)
        return remote(block, block, op_send.at[part, upper], op_recv.at[part, upper], to)

    def forward(part, k, half):
        if k in (2, 4):
            block = half_ref(half, part, shifted(axes_of(part)[2], 2), int(k == 4))
        else:
            block = block_ref(half, part, 2, shifted(axes_of(part)[2], 4 - k))
        return remote(block, block, fw_send.at[part, k], fw_recv.at[part, k], sibling)

    def peer_copy(q):
        return remote(peer_out.at[q], peer_in.at[q], pr_send.at[q], pr_recv.at[q], sibling)

    def half_terms(q, half):
        rows = cot[q].reshape(256, OWN * EDGE)
        return nt(rows, proj[pl.ds(pl.multiple_of(half * HALF, HALF), HALF), :])

    def scatter_first(part, r, k):
        groups = sum_groups(part)
        q = (me[0] + 1 + r) % 4
        if part == 0:
            return remote(
                terms.at[groups, q], slab1.at[r, groups],
                r0_send.at[0, r, 0], r0_recv.at[0, r, 0], device(shifted(0, 1 + r), core),
            )
        to = shifted(part, k)
        if part == 1:
            src = terms.at[groups, q, to[1]]
        else:
            src = terms.at[groups, q, :, to[2]]
        return remote(
            src, slab1.at[k - 1, groups, q],
            r0_send.at[part, r, k - 1], r0_recv.at[part, r, k - 1], device(to, core),
        )

    def peer_half(r):
        q = (me[0] + 1 + r) % 4
        peer_out[q] = half_terms(q, 1 - core).astype(BF16)
        peer_copy(q).start()

    def own_half(r):
        q = (me[0] + 1 + r) % 4
        total = half_terms(q, core)
        peer_copy(q).wait_recv()
        total = (total + peer_in[q].astype(F32)).astype(BF16)
        for g in range(GROUPS):
            terms[g, q] = total[:, g * 128 : (g + 1) * 128].reshape(4, 4, 16, 128)

    def send_terms(r):
        if r < 3:
            scatter_first(0, r, 0).start()
        for part in (1, 2):
            for k in STEPS:
                scatter_first(part, r, k).start()

    peer_half(0)
    blk_copy.wait_recv()
    theirs = blk_in[...]
    block16 = jnp.concatenate(
        [jnp.where(first, own_blk, theirs), jnp.where(first, theirs, own_blk)], axis=0
    ).astype(BF16)
    for g in range(GROUPS + 1):
        right[core, g, me[0], me[1], me[2]] = block16[:, g * 128 : (g + 1) * 128]
    for part in PARTS:
        for k in STEPS:
            gather(part, 0, k).start()

    proj_half(core)
    peer_half(1)
    own_half(0)
    send_terms(0)
    peer_half(2)
    for part in PARTS:
        for k in STEPS:
            gather(part, 0, k, True).wait_recv()
    for part in PARTS:
        for k in STEPS:
            gather(part, 1, k).start()
    own_half(1)
    send_terms(1)
    peer_half(3)
    own_half(2)
    send_terms(2)
    own_half(3)
    send_terms(3)
    edge_load.wait()
    for i in range(OWN):
        u_acc[:, :, :, :, i * EDGE : (i + 1) * EDGE] = edge[i].astype(F32)
    for part in PARTS:
        for k in STEPS:
            gather(part, 1, k, True).wait_recv()
    for part in PARTS:
        for k in (1, 3):
            gather(part, 2, k).start()
    for part in PARTS:
        forward(part, 0, core).start()

    def scatter(part, phase, k):
        axes = axes_of(part)
        groups = sum_groups(part)
        to = shifted(axes[phase], k)
        there = to[axes[phase]]
        if phase == 1:
            idx = [slice(None)] * 2
            idx[0 if axes[1] < axes[2] else 1] = there
            src, dst = sum1.at[groups, idx[0], idx[1]], slab2.at[k - 1, groups]
        else:
            src, dst = sum2.at[groups, there], slab3.at[k - 1, groups]
        return remote(
            src, dst, rs_send.at[part, phase - 1, k - 1], rs_recv.at[part, phase - 1, k - 1], device(to, core)
        )

    def scatter_add(part, phase):
        axes = axes_of(part)
        here = me[axes[phase]]
        first_group, count = 3 * part, 3 if part < 2 else GROUPS - 6
        if phase == 0:
            if part == 0:
                for r in range(3):
                    scatter_first(0, r, 0).wait_recv()
            else:
                for r in range(4):
                    for k in STEPS:
                        scatter_first(part, r, k).wait_recv()
        else:
            for k in STEPS:
                scatter(part, phase, k).wait_recv()
        for g in range(first_group, first_group + count):
            if phase == 0:
                idx = [slice(None)] * 3
                idx[axes[0]] = here
                total = terms[g, idx[0], idx[1], idx[2]].astype(F32)
                for k in range(3):
                    total += slab1[k, g].astype(F32)
                sum1[g] = total.astype(BF16)
            elif phase == 1:
                idx = [slice(None)] * 2
                idx[0 if axes[1] < axes[2] else 1] = here
                total = sum1[g, idx[0], idx[1]].astype(F32)
                for k in range(3):
                    total += slab2[k, g].astype(F32)
                sum2[g] = total.astype(BF16)
            else:
                total = sum2[g, here].astype(F32)
                for k in range(3):
                    total += slab3[k, g].astype(F32)
                fin_s[:, g * 128 : (g + 1) * 128] = total
        if phase < 2:
            for k in STEPS:
                scatter(part, phase + 1, k).start()

    def flat_plane(ref, lead, part, k):
        idx = plane_index(part, 2, shifted(axes_of(part)[2], (4 - k) % 4))
        return ref[lead + idx].reshape(256, ref.shape[-1])

    def count_of(part):
        return 3 if part < 2 else GROUPS - 6

    def left_plane(half, part, k):
        count = count_of(part)
        block = jnp.concatenate(
            [flat_plane(right, (half, 3 * part + n), part, k) for n in range(count)], axis=1
        )
        prod = lax.dot_general(
            block, flat_plane(cot, (), part, k), (((0,), (0,)), ((), ())), preferred_element_type=F32
        )
        rows = pl.ds(pl.multiple_of(half * HALF + part * 384, 128), count * 128)
        if k == 0:
            g_acc[rows, :] = prod
            return
        prod = prod + g_acc[rows, :]
        if k != 2:
            g_acc[rows, :] = prod
            return
        for n in range(count):
            gi = 3 * part + n
            for b in range(16):
                tile = prod[n * 128 + b * 8 : n * 128 + b * 8 + 8]
                lo = ((gi % 2) * 16 + b) * EDGE
                for m in range(OWN // 2):
                    pair = jnp.concatenate(
                        [tile[:, m * 256 : m * 256 + EDGE], tile[:, m * 256 + EDGE : m * 256 + 256]], axis=0
                    ).astype(BF16)
                    top = pl.multiple_of((half * 4 + gi // 2) * 64 + m * 16, 16)
                    gmat[pl.ds(top, 16), lo : lo + EDGE] = pair

    def pair_plane(part, k):
        count = count_of(part)
        lhs = jnp.concatenate(
            [flat_plane(right, (half, 3 * part + n), part, k) for half in range(2) for n in range(count)], axis=1
        )
        rhs = jnp.concatenate(
            [proj[half * HALF + part * 384 : half * HALF + part * 384 + count * 128, :] for half in range(2)], axis=0
        )
        u = jnp.dot(lhs, rhs, preferred_element_type=F32)
        idx = plane_index(part, 2, shifted(axes_of(part)[2], (4 - k) % 4))
        u_acc[idx] = u_acc[idx] + u.reshape(4, 4, 16, OWN * EDGE)

    def forwarded(k):
        for part in PARTS:
            forward(part, k, 1 - core).wait_recv()
            if k == 2:
                forward(part, 4, 1 - core).wait_recv()

    def left_own(k):
        for part in PARTS:
            left_plane(core, part, k)

    def left_other(k):
        for part in PARTS:
            left_plane(1 - core, part, k)

    def pair(k):
        for part in PARTS:
            pair_plane(part, k)

    def neighbours():
        for k in (1, 3):
            for part in PARTS:
                gather(part, 2, k, True).wait_recv()
                opposite(part, int(k == 3)).start()
                forward(part, k, core).start()

    def opposites():
        for part in PARTS:
            for upper in (0, 1):
                opposite(part, upper, True).wait_recv()
                forward(part, 2 + 2 * upper, core).start()

    def reduce(phase):
        for part in PARTS:
            scatter_add(part, phase)

    def left_gradient():
        gl = nt(gmat[...], wflat[...])
        for h in range(8):
            for i in range(OWN):
                tile = gl[h * 64 + i * 8 : h * 64 + i * 8 + 8] * (pad_ref[i].astype(F32) * (1.0 / SEQS))
                grad_s[pl.ds(h * 64 + i, 8, stride=OWN), :] = tile
        gn_ref[...] = jnp.dot(grad_s[...].astype(BF16), w1t_ref[...], preferred_element_type=F32)

    left_own(0)
    forwarded(0)
    left_other(0)
    pair(0)
    neighbours()
    left_own(1)
    left_own(3)
    reduce(0)
    forwarded(1)
    left_other(1)
    forwarded(3)
    left_other(3)
    opposites()
    pair(1)
    left_own(2)
    reduce(1)
    pair(3)
    forwarded(2)
    left_other(2)
    pair(2)
    for half in range(2):
        labels[half] = right[half, GROUPS]
    reduce(2)
    fin = fin_s[...]
    fin_out[...] = jnp.where(first, fin[8:], fin[:8])
    fin_mine = jnp.where(first, fin[:8], fin[8:])
    fin_copy = remote(fin_out, fin_in, misc_send.at[1], misc_recv.at[1], sibling)
    fin_copy.start()
    left_gradient()

    fin_copy.wait_recv()
    fin_theirs = fin_in[...]
    lo_half = jnp.where(first, fin_mine, fin_theirs) * keep_one
    hi_half = jnp.where(first, fin_theirs, fin_mine) * keep_one
    spread_rows = []
    for h in range(8):
        src = lo_half if h < 4 else hi_half
        base = src[:, (h % 4) * 256 : (h % 4) * 256 + 256]
        spread_rows.append(jnp.where(mine, base[None], 0.0).reshape(8 * OWN, FEAT))
    gr = jnp.concatenate(spread_rows, axis=0).astype(BF16)
    gn_ref[...] += jnp.dot(gr, w2e, preferred_element_type=F32)

    blk_copy.wait_send()
    fin_copy.wait_send()
    for part in PARTS:
        for k in STEPS:
            for phase in (1, 2):
                scatter(part, phase, k).wait_send()
            gather(part, 0, k).wait_send()
            gather(part, 1, k).wait_send()
        for k in (1, 3):
            gather(part, 2, k).wait_send()
        for upper in (0, 1):
            opposite(part, upper).wait_send()
        for k in range(5):
            forward(part, k, core).wait_send()
    for r in range(4):
        if r < 3:
            scatter_first(0, r, 0).wait_send()
        for part in (1, 2):
            for k in STEPS:
                scatter_first(part, r, k).wait_send()
        peer_copy(r).wait_send()


def finish_kernel(
    u_ref, labels, gn_ref, unit_ref, rstd_ref, gain_ref, off_ref, smo_ref, pad_ref, mol_ref,
    pair_out, grad_out, held, grad, sems,
):
    stores = [pltpu.make_async_copy(held.at[i], pair_out.at[i], sems.at[i]) for i in range(OWN)]
    grad_store = pltpu.make_async_copy(grad, grad_out, sems.at[OWN])
    keep_j = labels[0].astype(F32)
    mol_j = labels[1].astype(F32)
    apart = keep_j * off_ref[...]
    together = keep_j * (off_ref[...] + smo_ref[...])

    def pair(i):
        extra = jnp.where(mol_j == mol_ref[i].astype(F32), together, apart) * pad_ref[i].astype(F32)
        held[i] = (u_ref[:, i * EDGE : (i + 1) * EDGE] + extra).astype(BF16)
        stores[i].start()

    for i in range(4):
        pair(i)
    unit = unit_ref[...]
    gained = gn_ref[...] * gain_ref[...]
    result = rstd_ref[:, :1] * (
        gained
        - jnp.mean(gained, axis=-1, keepdims=True)
        - unit * jnp.mean(gained * unit, axis=-1, keepdims=True)
    )
    grad[...] = result.reshape(SEQS, OWN, FEAT)
    grad_store.start()
    for i in range(4, OWN):
        pair(i)
    for cp in stores:
        cp.wait()
    grad_store.wait()


def local(x, gain, w1, w2, wf, off, smo, edge, cot, pad, mol):
    vmem = pl.BlockSpec(memory_space=pltpu.VMEM)
    smem = pl.BlockSpec(memory_space=pltpu.SMEM)
    hbm = pl.BlockSpec(memory_space=pl.ANY)
    dma = pltpu.SemaphoreType.DMA
    gain = gain.reshape(1, FEAT)
    operands = (x, gain, w1.T, w2.T, wf) + tuple(
        v.reshape(OWN, 4, 4, 4, 16, EDGE) for v in (edge, cot)
    ) + (pad, mol)
    u, labels, gn, unit, rstd = pl.pallas_call(
        exchange_kernel,
        out_shape=(
            pltpu.VMEM((4, 4, 4, 16, OWN * EDGE), F32),
            pltpu.VMEM((2, 4, 4, 4, 16, 128), BF16),
            pltpu.VMEM((SEQS * OWN, FEAT), F32),
            pltpu.VMEM((SEQS * OWN, FEAT), F32),
            pltpu.VMEM((SEQS * OWN, 128), F32),
        ),
        in_specs=[hbm] * 9,
        out_specs=(vmem,) * 5,
        scratch_shapes=[
            pltpu.VMEM((SEQS, OWN, FEAT), BF16),
            pltpu.VMEM((1, FEAT), F32),
            pltpu.VMEM((FACTOR, FEAT), BF16),
            pltpu.VMEM((FACTOR, FEAT), BF16),
            pltpu.VMEM((FACTOR * FACTOR, EDGE), BF16),
            pltpu.SMEM((OWN,), jnp.int32),
            pltpu.SMEM((OWN,), jnp.int32),
            pltpu.VMEM((OWN, 4, 4, 4, 16, EDGE), BF16),
            pltpu.VMEM((4, 4, 4, 16, OWN * EDGE), BF16),
            pltpu.VMEM((2, GROUPS + 1, 4, 4, 4, 16, 128), BF16),
            pltpu.VMEM((2, OWN * 32, FACTOR), BF16),
            pltpu.VMEM((2 * HALF, OWN * EDGE), BF16),
            pltpu.VMEM((GROUPS, 4, 4, 4, 16, 128), BF16),
            pltpu.VMEM((4, 256, HALF), BF16),
            pltpu.VMEM((4, 256, HALF), BF16),
            pltpu.VMEM((3, GROUPS, 4, 4, 16, 128), BF16),
            pltpu.VMEM((GROUPS, 4, 4, 16, 128), BF16),
            pltpu.VMEM((3, GROUPS, 4, 16, 128), BF16),
            pltpu.VMEM((GROUPS, 4, 16, 128), BF16),
            pltpu.VMEM((3, GROUPS, 16, 128), BF16),
            pltpu.VMEM((2 * HALF, OWN * EDGE), F32),
            pltpu.VMEM((SEQS * OWN, FACTOR * EDGE), BF16),
            pltpu.VMEM((FACTOR * FACTOR, EDGE), F32),
            pltpu.VMEM((FACTOR, FACTOR * EDGE), BF16),
            pltpu.VMEM((SEQS * OWN, FACTOR), F32),
            pltpu.VMEM((SEQS * OWN, FACTOR), F32),
            pltpu.VMEM((OWN, HALF + 128), F32),
            pltpu.VMEM((OWN, HALF + 128), F32),
            pltpu.VMEM((16, HALF), F32),
            pltpu.VMEM((OWN, HALF), F32),
            pltpu.VMEM((OWN, HALF), F32),
            dma((OWN + 8,)),
            dma((3, 3, 3)),
            dma((3, 3, 3)),
            dma((3, 2)),
            dma((3, 2)),
            dma((3, 5)),
            dma((3, 5)),
            dma((3, 4, 3)),
            dma((3, 4, 3)),
            dma((3, 2, 3)),
            dma((3, 2, 3)),
            dma((4,)),
            dma((4,)),
            dma((2,)),
            dma((2,)),
        ],
        compiler_params=pltpu.CompilerParams(
            collective_id=0, has_side_effects=True, vmem_limit_bytes=50 * 2**20
        ),
        name="outer_product_mean",
    )(*(pltpu.with_memory_space_constraint(v, pltpu.HBM) for v in operands))
    return pl.pallas_call(
        finish_kernel,
        out_shape=(
            jax.ShapeDtypeStruct(edge.shape, BF16),
            jax.ShapeDtypeStruct(x.shape, F32),
        ),
        in_specs=[vmem] * 8 + [smem, smem],
        out_specs=(hbm, hbm),
        scratch_shapes=[
            pltpu.VMEM((OWN, LENGTH, EDGE), BF16),
            pltpu.VMEM((SEQS, OWN, FEAT), F32),
            dma((OWN + 1,)),
        ],
        compiler_params=pltpu.CompilerParams(vmem_limit_bytes=16 * 2**20),
        name="finish",
    )(
        u.reshape(LENGTH, OWN * EDGE), labels.reshape(2, LENGTH, 128), gn, unit, rstd, gain,
        off.reshape(1, EDGE), smo.reshape(1, EDGE), pad, mol,
    )


def solution(mesh):
    rows = ("branch", "res")
    return jax.shard_map(
        local,
        mesh=mesh,
        in_specs=(
            P(None, rows, None), P(), P(), P(), P(), P(), P(),
            P(rows, None, None), P(rows, None, None), P(rows), P(rows),
        ),
        out_specs=(P(rows, None, None), P(None, rows, None)),
        check_vma=False,
    )
```

```python
import jax
import jax.numpy as jnp
from jax import lax
from jax.experimental import pallas as pl
from jax.experimental.pallas import tpu as pltpu
from jax.sharding import PartitionSpec as P

MESH = pl.DeviceIdType.MESH
F32 = jnp.float32
BF16 = jnp.bfloat16

SEQS = 64
FEAT = 256
FACTOR = 32
EDGE = 128
LENGTH = 1024
OWN = 8
HALF = 1024
GROUPS = HALF // 128
EPSILON = 1e-05

PARTS = (0, 1, 2)
STEPS = (1, 2, 3)
FORWARD = (0, 1, 3, 2, 3)
PLANE = tuple((k, m) for k in range(4) for m in range(4) if k or m)


def axes_of(part):
    return (part % 3, (part + 1) % 3, (part + 2) % 3)


def sum_groups(part):
    return pl.ds(3 * part, 3 if part < 2 else GROUPS - 6)


def nt(a, b):
    return lax.dot_general(a, b, (((1,), (1,)), ((), ())), preferred_element_type=F32)


def normalise(x):
    xs = x.astype(F32).reshape(SEQS * OWN, FEAT)
    centred = xs - jnp.mean(xs, axis=-1, keepdims=True)
    rstd = lax.rsqrt(jnp.mean(centred * centred, axis=-1, keepdims=True) + EPSILON)
    return centred * rstd, rstd


def exchange_kernel(
    x_hbm, gain_hbm, w1t_hbm, w2t_hbm, wf_hbm, edge_hbm, cot_hbm, pad_hbm, mol_hbm,
    u_acc, labels, gn_ref, unit_ref, rstd_ref,
    x_ref, gain_ref, w1t_ref, w2t_ref, wf_ref, pad_ref, mol_ref,
    edge, cot, right, left_b, proj, terms, peer_out, peer_in, hop0, hop, slab1, sum1, slab2, sum2, slab3,
    g_acc, gmat, wff, wflat, left_s, grad_s, blk_out, blk_in, fin_s, fin_out, fin_in,
    load_sem,
    ag_send, ag_recv, nb_send, nb_recv, op_send, op_recv, fw_send, fw_recv,
    r0_send, r0_recv, rs_send, rs_recv, pr_send, pr_recv, misc_send, misc_recv,
):
    branch, res = lax.axis_index("branch"), lax.axis_index("res")
    core = res % 2
    first = core == 0
    me = (branch * 2 + res // 32, (res // 8) % 4, (res // 2) % 4)

    def device(at, c):
        return (at[0] // 2, (at[0] % 2) * 32 + at[1] * 8 + at[2] * 2 + c)

    def shifted(axis, k, other=None, m=0):
        at = list(me)
        at[axis] = (at[axis] + k) % 4
        if other is not None:
            at[other] = (at[other] + m) % 4
        return at

    def remote(src, dst, send, recv, to):
        return pltpu.make_async_remote_copy(src, dst, send, recv, device_id=to, device_id_type=MESH)

    sibling = device(me, 1 - core)

    def settle(send, recv, groups, rows, cols):
        block = right.at[0, pl.ds(0, groups), pl.ds(0, rows), pl.ds(0, cols), 0]
        return remote(block, block, send, recv, sibling)

    small = (
        (x_hbm, x_ref), (gain_hbm, gain_ref), (w2t_hbm, w2t_ref), (w1t_hbm, w1t_ref),
        (wf_hbm, wf_ref), (pad_hbm, pad_ref), (mol_hbm, mol_ref),
    )
    small_loads = [
        pltpu.make_async_copy(src, dst, load_sem.at[2 + n]) for n, (src, dst) in enumerate(small)
    ]
    for cp in small_loads:
        cp.start()

    barrier = pltpu.get_barrier_semaphore()
    for part in PARTS:
        axes = axes_of(part)
        for k in STEPS:
            for m in range(4):
                to = device(shifted(axes[0], k, axes[1], m), core)
                pl.semaphore_signal(barrier, inc=1, device_id=to, device_id_type=MESH)
    pl.semaphore_signal(barrier, inc=1, device_id=sibling, device_id_type=MESH)

    cot_loads = [
        pltpu.make_async_copy(cot_hbm.at[i], cot.at[:, :, :, :, pl.ds(i * EDGE, EDGE)], load_sem.at[0])
        for i in range(OWN)
    ]
    edge_load = pltpu.make_async_copy(edge_hbm, edge, load_sem.at[1])
    for cp in cot_loads:
        cp.start()
    edge_load.start()

    for cp in small_loads:
        cp.wait()
    unit, rstd = normalise(x_ref[...])
    unit_ref[...] = unit
    rstd_ref[...] = jnp.broadcast_to(rstd, rstd_ref.shape)
    normed = (unit * gain_ref[...]).astype(BF16)

    lane = lax.broadcasted_iota(jnp.int32, (FACTOR, FEAT), 1)
    row = lax.broadcasted_iota(jnp.int32, (FACTOR, FEAT), 0)
    spread = jnp.where(lane // 8 == row, 1.0, 0.0).astype(BF16)
    w2e = lax.dot_general(
        spread, w2t_ref[...], (((0,), (0,)), ((), ())), preferred_element_type=F32
    ).astype(BF16)

    rows8 = lax.broadcasted_iota(jnp.int32, (OWN, 128), 0)
    keep_col = jnp.zeros((OWN, 128), F32)
    mol_col = jnp.zeros((OWN, 128), F32)
    for i in range(OWN):
        keep_col = jnp.where(rows8 == i, pad_ref[i].astype(F32), keep_col)
        mol_col = jnp.where(rows8 == i, mol_ref[i].astype(F32), mol_col)
    keep_one = keep_col[:, :1]

    lane4 = lax.broadcasted_iota(jnp.int32, (8, OWN, FEAT), 2) % 8
    slot4 = lax.broadcasted_iota(jnp.int32, (8, OWN, FEAT), 0)
    mine = lane4 == slot4
    right_e = nt(normed, w2e).astype(BF16).astype(F32).reshape(8, 8, OWN, FEAT)
    flat = [jnp.sum(jnp.where(mine, right_e[h], 0.0), axis=0) * keep_one for h in range(8)]
    half0 = jnp.concatenate(flat[:4] + [keep_col], axis=1)
    half1 = jnp.concatenate(flat[4:] + [mol_col], axis=1)
    blk_out[...] = jnp.where(first, half1, half0)
    own_blk = jnp.where(first, half0, half1)

    pl.semaphore_wait(barrier, 37)
    blk_copy = remote(blk_out, blk_in, misc_send.at[0], misc_recv.at[0], sibling)
    blk_copy.start()

    left_s[...] = nt(normed, w1t_ref[...]).astype(BF16).astype(F32)
    wff[...] = wf_ref[...].astype(F32)
    for b in range(FACTOR):
        wflat[:, b * EDGE : (b + 1) * EDGE] = wff[pl.ds(b, FACTOR, stride=FACTOR), :].astype(BF16)
    for i in range(OWN):
        rows = left_s[pl.ds(i, SEQS, stride=OWN), :] * (pad_ref[i].astype(F32) * (1.0 / SEQS))
        for half in range(2):
            left_b[half, i * 32 : i * 32 + 32, :] = rows[half * 32 : half * 32 + 32].astype(BF16)

    def proj_half(half):
        left = left_b[half]

        def step(m, carry):
            for v in range(4):
                n = m * 4 + v
                y = jnp.dot(left, wflat[:, pl.ds(pl.multiple_of(n * 256, 256), 256)], preferred_element_type=F32)
                for i in range(OWN):
                    for h in range(4):
                        tile = y[i * 32 + h * 8 : i * 32 + h * 8 + 8]
                        pair = jnp.concatenate([tile[:, :EDGE], tile[:, EDGE:]], axis=0).astype(BF16)
                        top = pl.multiple_of(half * HALF + h * 256 + n * 16, 16)
                        proj[pl.ds(top, 16), i * EDGE : (i + 1) * EDGE] = pair
            return carry

        lax.fori_loop(0, 4, step, 0)

    def plane_index(part, phase, at):
        idx = list(at)
        for axis in axes_of(part)[:phase]:
            idx[axis] = slice(None)
        return tuple(idx)

    def block_ref(half, part, phase, at):
        return right.at[(half, pl.ds(3 * part, 3)) + plane_index(part, phase, at)]

    def half_ref(half, part, at, upper):
        idx = list(plane_index(part, 2, at))
        idx[axes_of(part)[0]] = pl.ds(2 * upper, 2)
        return right.at[(half, pl.ds(3 * part, 3)) + tuple(idx)]

    def scattered(part, k, m, receive=False):
        axes = axes_of(part)
        there = shifted(axes[0], (4 - k) % 4, axes[1], (4 - m) % 4)
        block = block_ref(core, part, 0, there if receive else me)
        to = device(there if receive else shifted(axes[0], k, axes[1], m), core)
        return remote(block, block, ag_send.at[part], ag_recv.at[part], to)

    def neighbour(part, k, receive=False):
        axis = axes_of(part)[2]
        at = shifted(axis, 4 - k) if receive else me
        block = block_ref(core, part, 2, at)
        to = device(shifted(axis, 4 - k if receive else k), core)
        return remote(block, block, nb_send.at[part], nb_recv.at[part], to)

    def opposite(part, upper, receive=False):
        axis = axes_of(part)[2]
        k = 3 if upper else 1
        at = shifted(axis, 2) if receive else shifted(axis, 4 - k)
        block = half_ref(core, part, at, upper)
        to = device(shifted(axis, 4 - k if receive else k), core)
        return remote(block, block, op_send.at[part], op_recv.at[part], to)

    def forward(part, k, half):
        if k in (2, 4):
            block = half_ref(half, part, shifted(axes_of(part)[2], 2), int(k == 4))
        else:
            block = block_ref(half, part, 2, shifted(axes_of(part)[2], 4 - k))
        return remote(block, block, fw_send.at[FORWARD[k]], fw_recv.at[FORWARD[k]], sibling)

    def peer_copy(q):
        return remote(peer_out.at[q], peer_in.at[q], pr_send.at[q], pr_recv.at[q], sibling)

    def half_terms(q, half):
        rows = cot[q].reshape(256, OWN * EDGE)
        return nt(rows, proj[pl.ds(pl.multiple_of(half * HALF, HALF), HALF), :])

    def quarter(r):
        return (me[0] + (2, 1, 3, 0)[r]) % 4

    def hop_first(upper):
        groups = sum_groups(0)
        return remote(
            terms.at[groups, quarter(0), pl.ds(2 * upper, 2)], hop0.at[upper, groups],
            r0_send.at[upper], r0_recv.at[upper], device(shifted(0, 3 if upper else 1), core),
        )

    def slab_first(r):
        groups = sum_groups(0)
        return remote(
            terms.at[groups, quarter(r)], slab1.at[r - 1, groups],
            r0_send.at[2], r0_recv.at[2], device(shifted(0, 1 if r == 1 else 3), core),
        )

    def scatter_first(part, r, what):
        groups, q = sum_groups(part), quarter(r)
        up = r % 2 == 0 if what == 0 else what == 1
        there = shifted(part, 2 if what == 0 else (1 if up else 3))
        if part == 1:
            src = terms.at[groups, q, there[1]]
        else:
            src = terms.at[groups, q, :, there[2]]
        dst = hop.at[part - 1, q, groups] if what == 0 else slab1.at[what - 1, groups, q]
        sem = 3 + r if what == 0 else 6 + part
        return remote(
            src, dst, r0_send.at[sem], r0_recv.at[sem],
            device(shifted(part, 1 if up else 3), core),
        )

    def combine(r):
        q = quarter(r)
        what = 1 if r % 2 == 0 else 2
        settle(r0_send.at[3 + r], r0_recv.at[3 + r], 5, 4, 1).wait_recv()
        for part in (1, 2):
            there = shifted(part, 1 if what == 1 else 3)
            for g in range(3 * part, 3 * part + (3 if part < 2 else GROUPS - 6)):
                idx = (g, q, there[1]) if part == 1 else (g, q, slice(None), there[2])
                terms[idx] = (terms[idx].astype(F32) + hop[part - 1, q, g].astype(F32)).astype(BF16)
            scatter_first(part, r, what).start()

    def peer_half(r):
        q = quarter(r)
        peer_out[q] = half_terms(q, 1 - core).astype(BF16)
        peer_copy(q).start()

    def own_half(r):
        q = quarter(r)
        total = half_terms(q, core)
        peer_copy(q).wait_recv()
        total = (total + peer_in[q].astype(F32)).astype(BF16)
        for g in range(GROUPS):
            terms[g, q] = total[:, g * 128 : (g + 1) * 128].reshape(4, 4, 16, 128)

    def send_terms(r):
        if r == 0:
            for upper in (0, 1):
                hop_first(upper).start()
        for part in (1, 2):
            scatter_first(part, r, 0).start()
            scatter_first(part, r, 2 if r % 2 == 0 else 1).start()

    def combine_first(r):
        upper = r - 1
        hop_first(upper).wait_recv()
        for g in range(3):
            idx = (g, quarter(r), pl.ds(2 * upper, 2))
            terms[idx] = (terms[idx].astype(F32) + hop0[upper, g].astype(F32)).astype(BF16)
        slab_first(r).start()

    blk_copy.wait_recv()
    theirs = blk_in[...]
    block16 = jnp.concatenate(
        [jnp.where(first, own_blk, theirs), jnp.where(first, theirs, own_blk)], axis=0
    ).astype(BF16)
    for g in range(GROUPS + 1):
        right[core, g, me[0], me[1], me[2]] = block16[:, g * 128 : (g + 1) * 128]
    for k, m in PLANE:
        for part in PARTS:
            scattered(part, k, m).start()

    proj_half(1 - core)
    pltpu.make_async_copy(cot, cot, load_sem.at[0]).wait()
    peer_half(0)
    proj_half(core)
    peer_half(1)
    own_half(0)
    send_terms(0)
    peer_half(2)
    own_half(1)
    send_terms(1)
    for part in PARTS:
        settle(ag_send.at[part], ag_recv.at[part], 5, 3, 3).wait_recv()
    for part in PARTS:
        for k in (1, 3):
            neighbour(part, k).start()
    for part in PARTS:
        forward(part, 0, core).start()
    peer_half(3)
    own_half(2)
    send_terms(2)
    own_half(3)
    send_terms(3)
    combine_first(1)
    combine(0)
    edge_load.wait()
    for i in range(OWN):
        u_acc[:, :, :, :, i * EDGE : (i + 1) * EDGE] = edge[i].astype(F32)

    def scatter(part, phase, k):
        axes = axes_of(part)
        groups = sum_groups(part)
        to = shifted(axes[phase], k)
        there = to[axes[phase]]
        if phase == 1:
            idx = [slice(None)] * 2
            idx[0 if axes[1] < axes[2] else 1] = there
            src, dst = sum1.at[groups, idx[0], idx[1]], slab2.at[k - 1, groups]
        else:
            src, dst = sum2.at[groups, there], slab3.at[k - 1, groups]
        return remote(
            src, dst, rs_send.at[part, phase - 1], rs_recv.at[part, phase - 1], device(to, core)
        )

    def settled(part, phase):
        send, recv = rs_send.at[part, phase - 1], rs_recv.at[part, phase - 1]
        return settle(send, recv, 9 if part < 2 else 6, 4 if phase == 1 else 1, 1)

    def scatter_add(part, phase):
        axes = axes_of(part)
        here = me[axes[phase]]
        first_group, count = 3 * part, 3 if part < 2 else GROUPS - 6
        if phase == 0:
            sem, tiles = ((2, (6, 4, 4)), (7, (6, 4, 4)), (8, (4, 4, 4)))[part]
            settle(r0_send.at[sem], r0_recv.at[sem], *tiles).wait_recv()
        else:
            settled(part, phase).wait_recv()
        for g in range(first_group, first_group + count):
            if phase == 0:
                idx = [slice(None)] * 3
                idx[axes[0]] = here
                total = terms[g, idx[0], idx[1], idx[2]].astype(F32)
                for k in range(2):
                    total += slab1[k, g].astype(F32)
                sum1[g] = total.astype(BF16)
            elif phase == 1:
                idx = [slice(None)] * 2
                idx[0 if axes[1] < axes[2] else 1] = here
                total = sum1[g, idx[0], idx[1]].astype(F32)
                for k in range(3):
                    total += slab2[k, g].astype(F32)
                sum2[g] = total.astype(BF16)
            else:
                total = sum2[g, here].astype(F32)
                for k in range(3):
                    total += slab3[k, g].astype(F32)
                fin_s[:, g * 128 : (g + 1) * 128] = total
        if phase < 2:
            for k in STEPS:
                scatter(part, phase + 1, k).start()

    def flat_plane(ref, lead, part, k):
        idx = plane_index(part, 2, shifted(axes_of(part)[2], (4 - k) % 4))
        return ref[lead + idx].reshape(256, ref.shape[-1])

    def count_of(part):
        return 3 if part < 2 else GROUPS - 6

    def left_plane(half, part, k):
        count = count_of(part)
        block = jnp.concatenate(
            [flat_plane(right, (half, 3 * part + n), part, k) for n in range(count)], axis=1
        )
        prod = lax.dot_general(
            block, flat_plane(cot, (), part, k), (((0,), (0,)), ((), ())), preferred_element_type=F32
        )
        rows = pl.ds(pl.multiple_of(half * HALF + part * 384, 128), count * 128)
        if k == 0:
            g_acc[rows, :] = prod
            return
        prod = prod + g_acc[rows, :]
        if k != 2:
            g_acc[rows, :] = prod
            return
        for n in range(count):
            gi = 3 * part + n
            for b in range(16):
                tile = prod[n * 128 + b * 8 : n * 128 + b * 8 + 8]
                lo = ((gi % 2) * 16 + b) * EDGE
                for m in range(OWN // 2):
                    pair = jnp.concatenate(
                        [tile[:, m * 256 : m * 256 + EDGE], tile[:, m * 256 + EDGE : m * 256 + 256]], axis=0
                    ).astype(BF16)
                    top = pl.multiple_of((half * 4 + gi // 2) * 64 + m * 16, 16)
                    gmat[pl.ds(top, 16), lo : lo + EDGE] = pair

    def pair_plane(part, k):
        count = count_of(part)
        lhs = jnp.concatenate(
            [flat_plane(right, (half, 3 * part + n), part, k) for half in range(2) for n in range(count)], axis=1
        )
        rhs = jnp.concatenate(
            [proj[half * HALF + part * 384 : half * HALF + part * 384 + count * 128, :] for half in range(2)], axis=0
        )
        u = jnp.dot(lhs, rhs, preferred_element_type=F32)
        idx = plane_index(part, 2, shifted(axes_of(part)[2], (4 - k) % 4))
        u_acc[idx] = u_acc[idx] + u.reshape(4, 4, 16, OWN * EDGE)

    def forwarded(k):
        settle(fw_send.at[FORWARD[k]], fw_recv.at[FORWARD[k]], 9, 4, 4).wait_recv()

    def left_own(k):
        for part in PARTS:
            left_plane(core, part, k)

    def left_other(k):
        for part in PARTS:
            left_plane(1 - core, part, k)

    def pair(k):
        for part in PARTS:
            pair_plane(part, k)

    def neighbours():
        for part in PARTS:
            settle(nb_send.at[part], nb_recv.at[part], 6, 4, 4).wait_recv()
            for k in (1, 3):
                opposite(part, int(k == 3)).start()
        for k in (1, 3):
            for part in PARTS:
                forward(part, k, core).start()

    def opposites():
        for part in PARTS:
            settle(op_send.at[part], op_recv.at[part], 3, 4, 4).wait_recv()
            for upper in (0, 1):
                forward(part, 2 + 2 * upper, core).start()

    def reduce(phase):
        for part in PARTS:
            scatter_add(part, phase)

    def left_gradient():
        gl = nt(gmat[...], wflat[...])
        for h in range(8):
            for i in range(OWN):
                tile = gl[h * 64 + i * 8 : h * 64 + i * 8 + 8] * (pad_ref[i].astype(F32) * (1.0 / SEQS))
                grad_s[pl.ds(h * 64 + i, 8, stride=OWN), :] = tile
        gn_ref[...] = jnp.dot(grad_s[...].astype(BF16), w1t_ref[...], preferred_element_type=F32)

    left_own(0)
    combine(1)
    combine_first(2)
    forwarded(0)
    left_other(0)
    combine(2)
    pair(0)
    combine(3)
    neighbours()
    left_own(1)
    left_own(3)
    reduce(0)
    forwarded(1)
    left_other(1)
    forwarded(3)
    left_other(3)
    opposites()
    pair(1)
    left_own(2)
    reduce(1)
    pair(3)
    forwarded(2)
    left_other(2)
    pair(2)
    for half in range(2):
        labels[half] = right[half, GROUPS]
    reduce(2)
    fin = fin_s[...]
    fin_out[...] = jnp.where(first, fin[8:], fin[:8])
    fin_mine = jnp.where(first, fin[:8], fin[8:])
    fin_copy = remote(fin_out, fin_in, misc_send.at[1], misc_recv.at[1], sibling)
    fin_copy.start()
    left_gradient()

    fin_copy.wait_recv()
    fin_theirs = fin_in[...]
    lo_half = jnp.where(first, fin_mine, fin_theirs) * keep_one
    hi_half = jnp.where(first, fin_theirs, fin_mine) * keep_one
    spread_rows = []
    for h in range(8):
        src = lo_half if h < 4 else hi_half
        base = src[:, (h % 4) * 256 : (h % 4) * 256 + 256]
        spread_rows.append(jnp.where(mine, base[None], 0.0).reshape(8 * OWN, FEAT))
    gr = jnp.concatenate(spread_rows, axis=0).astype(BF16)
    gn_ref[...] += jnp.dot(gr, w2e, preferred_element_type=F32)

    blk_copy.wait_send()
    fin_copy.wait_send()
    for part in PARTS:
        for phase in (1, 2):
            settled(part, phase).wait_send()
        settle(ag_send.at[part], ag_recv.at[part], 5, 3, 3).wait_send()
        settle(nb_send.at[part], nb_recv.at[part], 6, 4, 4).wait_send()
        settle(op_send.at[part], op_recv.at[part], 3, 4, 4).wait_send()
    for k in range(4):
        settle(fw_send.at[k], fw_recv.at[k], 9, 4, 4).wait_send()
    for r in range(4):
        settle(r0_send.at[3 + r], r0_recv.at[3 + r], 5, 4, 1).wait_send()
        peer_copy(r).wait_send()
    for sem, tiles in ((2, (6, 4, 4)), (7, (6, 4, 4)), (8, (4, 4, 4))):
        settle(r0_send.at[sem], r0_recv.at[sem], *tiles).wait_send()
    for upper in (0, 1):
        hop_first(upper).wait_send()


def finish_kernel(
    u_ref, labels, gn_ref, unit_ref, rstd_ref, gain_ref, off_ref, smo_ref, pad_ref, mol_ref,
    pair_out, grad_out, held, grad, sems,
):
    def store(q):
        rows = pl.ds(q * 256, 256)
        return pltpu.make_async_copy(held.at[:, rows], pair_out.at[:, rows], sems.at[q])

    grad_store = pltpu.make_async_copy(grad, grad_out, sems.at[4])

    def pair(q):
        for lo in range(q * 256, q * 256 + 256, 64):
            rows = slice(lo, lo + 64)
            keep_j = labels[0, rows, :].astype(F32)
            mol_j = labels[1, rows, :].astype(F32)
            apart = keep_j * off_ref[...]
            together = keep_j * (off_ref[...] + smo_ref[...])
            for i in range(OWN):
                extra = jnp.where(mol_j == mol_ref[i].astype(F32), together, apart) * pad_ref[i].astype(F32)
                held[i, rows, :] = (u_ref[rows, i * EDGE : (i + 1) * EDGE] + extra).astype(BF16)
        store(q).start()

    pair(0)
    pair(1)
    unit = unit_ref[...]
    gained = gn_ref[...] * gain_ref[...]
    result = rstd_ref[:, :1] * (
        gained
        - jnp.mean(gained, axis=-1, keepdims=True)
        - unit * jnp.mean(gained * unit, axis=-1, keepdims=True)
    )
    grad[...] = result.reshape(SEQS, OWN, FEAT)
    grad_store.start()
    pair(2)
    pair(3)
    for q in range(4):
        store(q).wait()
    grad_store.wait()


def local(x, gain, w1, w2, wf, off, smo, edge, cot, pad, mol):
    vmem = pl.BlockSpec(memory_space=pltpu.VMEM)
    smem = pl.BlockSpec(memory_space=pltpu.SMEM)
    hbm = pl.BlockSpec(memory_space=pl.ANY)
    dma = pltpu.SemaphoreType.DMA
    gain = gain.reshape(1, FEAT)
    operands = (x, gain, w1.T, w2.T, wf) + tuple(
        v.reshape(OWN, 4, 4, 4, 16, EDGE) for v in (edge, cot)
    ) + (pad, mol)
    u, labels, gn, unit, rstd = pl.pallas_call(
        exchange_kernel,
        out_shape=(
            pltpu.VMEM((4, 4, 4, 16, OWN * EDGE), F32),
            pltpu.VMEM((2, 4, 4, 4, 16, 128), BF16),
            pltpu.VMEM((SEQS * OWN, FEAT), F32),
            pltpu.VMEM((SEQS * OWN, FEAT), F32),
            pltpu.VMEM((SEQS * OWN, 128), F32),
        ),
        in_specs=[hbm] * 9,
        out_specs=(vmem,) * 5,
        scratch_shapes=[
            pltpu.VMEM((SEQS, OWN, FEAT), BF16),
            pltpu.VMEM((1, FEAT), F32),
            pltpu.VMEM((FACTOR, FEAT), BF16),
            pltpu.VMEM((FACTOR, FEAT), BF16),
            pltpu.VMEM((FACTOR * FACTOR, EDGE), BF16),
            pltpu.SMEM((OWN,), jnp.int32),
            pltpu.SMEM((OWN,), jnp.int32),
            pltpu.VMEM((OWN, 4, 4, 4, 16, EDGE), BF16),
            pltpu.VMEM((4, 4, 4, 16, OWN * EDGE), BF16),
            pltpu.VMEM((2, GROUPS + 1, 4, 4, 4, 16, 128), BF16),
            pltpu.VMEM((2, OWN * 32, FACTOR), BF16),
            pltpu.VMEM((2 * HALF, OWN * EDGE), BF16),
            pltpu.VMEM((GROUPS, 4, 4, 4, 16, 128), BF16),
            pltpu.VMEM((4, 256, HALF), BF16),
            pltpu.VMEM((4, 256, HALF), BF16),
            pltpu.VMEM((2, 3, 2, 4, 16, 128), BF16),
            pltpu.VMEM((2, 4, GROUPS, 4, 16, 128), BF16),
            pltpu.VMEM((2, GROUPS, 4, 4, 16, 128), BF16),
            pltpu.VMEM((GROUPS, 4, 4, 16, 128), BF16),
            pltpu.VMEM((3, GROUPS, 4, 16, 128), BF16),
            pltpu.VMEM((GROUPS, 4, 16, 128), BF16),
            pltpu.VMEM((3, GROUPS, 16, 128), BF16),
            pltpu.VMEM((2 * HALF, OWN * EDGE), F32),
            pltpu.VMEM((SEQS * OWN, FACTOR * EDGE), BF16),
            pltpu.VMEM((FACTOR * FACTOR, EDGE), F32),
            pltpu.VMEM((FACTOR, FACTOR * EDGE), BF16),
            pltpu.VMEM((SEQS * OWN, FACTOR), F32),
            pltpu.VMEM((SEQS * OWN, FACTOR), F32),
            pltpu.VMEM((OWN, HALF + 128), F32),
            pltpu.VMEM((OWN, HALF + 128), F32),
            pltpu.VMEM((16, HALF), F32),
            pltpu.VMEM((OWN, HALF), F32),
            pltpu.VMEM((OWN, HALF), F32),
            dma((9,)),
            dma((3,)),
            dma((3,)),
            dma((3,)),
            dma((3,)),
            dma((3,)),
            dma((3,)),
            dma((4,)),
            dma((4,)),
            dma((9,)),
            dma((9,)),
            dma((3, 2)),
            dma((3, 2)),
            dma((4,)),
            dma((4,)),
            dma((2,)),
            dma((2,)),
        ],
        compiler_params=pltpu.CompilerParams(
            collective_id=0, has_side_effects=True, vmem_limit_bytes=50 * 2**20
        ),
        name="outer_product_mean",
    )(*(pltpu.with_memory_space_constraint(v, pltpu.HBM) for v in operands))
    return pl.pallas_call(
        finish_kernel,
        out_shape=(
            jax.ShapeDtypeStruct(edge.shape, BF16),
            jax.ShapeDtypeStruct(x.shape, F32),
        ),
        in_specs=[vmem] * 8 + [smem, smem],
        out_specs=(hbm, hbm),
        scratch_shapes=[
            pltpu.VMEM((OWN, LENGTH, EDGE), BF16),
            pltpu.VMEM((SEQS, OWN, FEAT), F32),
            dma((5,)),
        ],
        compiler_params=pltpu.CompilerParams(vmem_limit_bytes=16 * 2**20),
        name="finish",
    )(
        u.reshape(LENGTH, OWN * EDGE), labels.reshape(2, LENGTH, 128), gn, unit, rstd, gain,
        off.reshape(1, EDGE), smo.reshape(1, EDGE), pad, mol,
    )


def solution(mesh):
    rows = ("branch", "res")
    return jax.shard_map(
        local,
        mesh=mesh,
        in_specs=(
            P(None, rows, None), P(), P(), P(), P(), P(), P(),
            P(rows, None, None), P(rows, None, None), P(rows), P(rows),
        ),
        out_specs=(P(rows, None, None), P(None, rows, None)),
        check_vma=False,
    )
```

```python
import jax
import jax.numpy as jnp
from jax import lax
from jax.experimental import pallas as pl
from jax.experimental.pallas import tpu as pltpu
from jax.sharding import PartitionSpec as P

MESH = pl.DeviceIdType.MESH
F32 = jnp.float32
BF16 = jnp.bfloat16

SEQS = 64
FEAT = 256
FACTOR = 32
EDGE = 128
LENGTH = 1024
OWN = 8
HALF = 1024
GROUPS = HALF // 128
EPSILON = 1e-05

PARTS = (0, 1, 2)
STEPS = (1, 2, 3)
FORWARD = (0, 1, 3, 2, 3)
DIRECT = (2, 3)
PLANE = tuple((k, m) for k in range(4) for m in range(4) if k or m)


def axes_of(part):
    return (part % 3, (part + 1) % 3, (part + 2) % 3)


def sum_groups(part):
    return pl.ds(3 * part, 3 if part < 2 else GROUPS - 6)


def nt(a, b):
    return lax.dot_general(a, b, (((1,), (1,)), ((), ())), preferred_element_type=F32)


def normalise(x):
    xs = x.astype(F32).reshape(SEQS * OWN, FEAT)
    centred = xs - jnp.mean(xs, axis=-1, keepdims=True)
    rstd = lax.rsqrt(jnp.mean(centred * centred, axis=-1, keepdims=True) + EPSILON)
    return centred * rstd, rstd


def exchange_kernel(
    x_hbm, gain_hbm, w1t_hbm, w2t_hbm, wf_hbm, edge_hbm, cot_hbm, pad_hbm, mol_hbm,
    u_acc, labels, gn_ref, unit_ref, rstd_ref,
    x_ref, gain_ref, w1t_ref, w2t_ref, wf_ref, pad_ref, mol_ref,
    edge, cot, right, left_b, proj, terms, peer_out, peer_in, hop0, hop, slab1, sum1, slab2, sum2, slab3,
    g_acc, gmat, wff, wflat, left_s, grad_s, blk_out, blk_in, fin_s, fin_out, fin_in,
    load_sem,
    ag_send, ag_recv, nb_send, nb_recv, op_send, op_recv, fw_send, fw_recv,
    r0_send, r0_recv, rs_send, rs_recv, pr_send, pr_recv, misc_send, misc_recv,
):
    branch, res = lax.axis_index("branch"), lax.axis_index("res")
    core = res % 2
    first = core == 0
    me = (branch * 2 + res // 32, (res // 8) % 4, (res // 2) % 4)

    def device(at, c):
        return (at[0] // 2, (at[0] % 2) * 32 + at[1] * 8 + at[2] * 2 + c)

    def shifted(axis, k, other=None, m=0):
        at = list(me)
        at[axis] = (at[axis] + k) % 4
        if other is not None:
            at[other] = (at[other] + m) % 4
        return at

    def remote(src, dst, send, recv, to):
        return pltpu.make_async_remote_copy(src, dst, send, recv, device_id=to, device_id_type=MESH)

    sibling = device(me, 1 - core)

    def settle(send, recv, groups, rows, cols):
        block = right.at[0, pl.ds(0, groups), pl.ds(0, rows), pl.ds(0, cols), 0]
        return remote(block, block, send, recv, sibling)

    small = (
        (x_hbm, x_ref), (gain_hbm, gain_ref), (w2t_hbm, w2t_ref), (w1t_hbm, w1t_ref),
        (wf_hbm, wf_ref), (pad_hbm, pad_ref), (mol_hbm, mol_ref),
    )
    small_loads = [
        pltpu.make_async_copy(src, dst, load_sem.at[2 + n]) for n, (src, dst) in enumerate(small)
    ]
    for cp in small_loads:
        cp.start()

    barrier = pltpu.get_barrier_semaphore()
    for part in PARTS:
        axes = axes_of(part)
        for k in STEPS:
            for m in range(4):
                to = device(shifted(axes[0], k, axes[1], m), core)
                pl.semaphore_signal(barrier, inc=1, device_id=to, device_id_type=MESH)
    pl.semaphore_signal(barrier, inc=1, device_id=sibling, device_id_type=MESH)

    cot_loads = [
        pltpu.make_async_copy(cot_hbm.at[i], cot.at[:, :, :, :, pl.ds(i * EDGE, EDGE)], load_sem.at[0])
        for i in range(OWN)
    ]
    edge_load = pltpu.make_async_copy(edge_hbm, edge, load_sem.at[1])
    for cp in cot_loads:
        cp.start()
    edge_load.start()

    for cp in small_loads:
        cp.wait()
    unit, rstd = normalise(x_ref[...])
    unit_ref[...] = unit
    rstd_ref[...] = jnp.broadcast_to(rstd, rstd_ref.shape)
    normed = (unit * gain_ref[...]).astype(BF16)

    lane = lax.broadcasted_iota(jnp.int32, (FACTOR, FEAT), 1)
    row = lax.broadcasted_iota(jnp.int32, (FACTOR, FEAT), 0)
    spread = jnp.where(lane // 8 == row, 1.0, 0.0).astype(BF16)
    w2e = lax.dot_general(
        spread, w2t_ref[...], (((0,), (0,)), ((), ())), preferred_element_type=F32
    ).astype(BF16)

    rows8 = lax.broadcasted_iota(jnp.int32, (OWN, 128), 0)
    keep_col = jnp.zeros((OWN, 128), F32)
    mol_col = jnp.zeros((OWN, 128), F32)
    for i in range(OWN):
        keep_col = jnp.where(rows8 == i, pad_ref[i].astype(F32), keep_col)
        mol_col = jnp.where(rows8 == i, mol_ref[i].astype(F32), mol_col)
    keep_one = keep_col[:, :1]

    lane4 = lax.broadcasted_iota(jnp.int32, (8, OWN, FEAT), 2) % 8
    slot4 = lax.broadcasted_iota(jnp.int32, (8, OWN, FEAT), 0)
    mine = lane4 == slot4
    right_e = nt(normed, w2e).astype(BF16).astype(F32).reshape(8, 8, OWN, FEAT)
    flat = [jnp.sum(jnp.where(mine, right_e[h], 0.0), axis=0) * keep_one for h in range(8)]
    half0 = jnp.concatenate(flat[:4] + [keep_col], axis=1)
    half1 = jnp.concatenate(flat[4:] + [mol_col], axis=1)
    blk_out[...] = jnp.where(first, half1, half0)
    own_blk = jnp.where(first, half0, half1)

    left_s[...] = nt(normed, w1t_ref[...]).astype(BF16).astype(F32)
    wff[...] = wf_ref[...].astype(F32)
    for b in range(FACTOR):
        wflat[:, b * EDGE : (b + 1) * EDGE] = wff[pl.ds(b, FACTOR, stride=FACTOR), :].astype(BF16)
    for i in range(OWN):
        rows = left_s[pl.ds(i, SEQS, stride=OWN), :] * (pad_ref[i].astype(F32) * (1.0 / SEQS))
        left_b[i * SEQS : (i + 1) * SEQS, :] = rows.astype(BF16)

    def proj_steps(start, stop):
        left = left_b[...]

        def step(m, carry):
            for v in range(4):
                n = m * 4 + v
                y = jnp.dot(left, wflat[:, pl.ds(pl.multiple_of(n * 256, 256), 256)], preferred_element_type=F32)
                for i in range(OWN):
                    for h in range(8):
                        tile = y[i * SEQS + h * 8 : i * SEQS + h * 8 + 8]
                        pair = jnp.concatenate([tile[:, :EDGE], tile[:, EDGE:]], axis=0).astype(BF16)
                        top = pl.multiple_of(h * 256 + n * 16, 16)
                        proj[pl.ds(top, 16), i * EDGE : (i + 1) * EDGE] = pair
            return carry

        lax.fori_loop(start, stop, step, 0)

    pl.semaphore_wait(barrier, 37)
    blk_copy = remote(blk_out, blk_in, misc_send.at[0], misc_recv.at[0], sibling)
    blk_copy.start()

    def plane_index(part, phase, at):
        idx = list(at)
        for axis in axes_of(part)[:phase]:
            idx[axis] = slice(None)
        return tuple(idx)

    def block_ref(half, part, phase, at):
        return right.at[(half, pl.ds(3 * part, 3)) + plane_index(part, phase, at)]

    def half_ref(half, part, at, upper):
        idx = list(plane_index(part, 2, at))
        idx[axes_of(part)[0]] = pl.ds(2 * upper, 2)
        return right.at[(half, pl.ds(3 * part, 3)) + tuple(idx)]

    def scattered(part, k, m, receive=False):
        axes = axes_of(part)
        there = shifted(axes[0], (4 - k) % 4, axes[1], (4 - m) % 4)
        block = block_ref(core, part, 0, there if receive else me)
        to = device(there if receive else shifted(axes[0], k, axes[1], m), core)
        return remote(block, block, ag_send.at[part], ag_recv.at[part], to)

    def neighbour(part, k, receive=False):
        axis = axes_of(part)[2]
        at = shifted(axis, 4 - k) if receive else me
        block = block_ref(core, part, 2, at)
        to = device(shifted(axis, 4 - k if receive else k), core)
        return remote(block, block, nb_send.at[part], nb_recv.at[part], to)

    def opposite(part, upper, receive=False):
        axis = axes_of(part)[2]
        k = 3 if upper else 1
        at = shifted(axis, 2) if receive else shifted(axis, 4 - k)
        block = half_ref(core, part, at, upper)
        to = device(shifted(axis, 4 - k if receive else k), core)
        return remote(block, block, op_send.at[part], op_recv.at[part], to)

    def forward(part, k, half):
        if k in (2, 4):
            block = half_ref(half, part, shifted(axes_of(part)[2], 2), int(k == 4))
        else:
            block = block_ref(half, part, 2, shifted(axes_of(part)[2], 4 - k))
        return remote(block, block, fw_send.at[FORWARD[k]], fw_recv.at[FORWARD[k]], sibling)

    def peer_copy(q):
        return remote(peer_out.at[q], peer_in.at[q], pr_send.at[q], pr_recv.at[q], sibling)

    def half_terms(q, half):
        rows = cot[q].reshape(256, OWN * EDGE)
        return nt(rows, proj[pl.ds(pl.multiple_of(half * HALF, HALF), HALF), :])

    def quarter(r):
        return (me[0] + (2, 1, 3, 0)[r]) % 4

    def hop_first(upper):
        groups = sum_groups(0)
        return remote(
            terms.at[groups, quarter(0), pl.ds(2 * upper, 2)], hop0.at[upper, groups],
            r0_send.at[upper], r0_recv.at[upper], device(shifted(0, 3 if upper else 1), core),
        )

    def slab_first(r):
        groups = sum_groups(0)
        return remote(
            terms.at[groups, quarter(r)], slab1.at[r - 1, groups],
            r0_send.at[2], r0_recv.at[2], device(shifted(0, 1 if r == 1 else 3), core),
        )

    def scatter_first(part, r, what):
        groups, q = sum_groups(part), quarter(r)
        up = r % 2 == 0 if what == 0 else what == 1
        there = shifted(part, 2 if what == 0 else (1 if up else 3))
        if part == 1:
            src = terms.at[groups, q, there[1]]
        else:
            src = terms.at[groups, q, :, there[2]]
        dst = hop.at[part - 1, q, groups] if what == 0 else slab1.at[what - 1, groups, q]
        sem = 3 + r if what == 0 else 6 + part
        return remote(
            src, dst, r0_send.at[sem], r0_recv.at[sem],
            device(there if what == 0 and r in DIRECT else shifted(part, 1 if up else 3), core),
        )

    def combine(r):
        q = quarter(r)
        what = 1 if r % 2 == 0 else 2
        settle(r0_send.at[3 + r], r0_recv.at[3 + r], 5, 4, 1).wait_recv()
        for part in (1, 2):
            there = shifted(part, 1 if what == 1 else 3)
            for g in range(3 * part, 3 * part + (3 if part < 2 else GROUPS - 6)):
                idx = (g, q, there[1]) if part == 1 else (g, q, slice(None), there[2])
                terms[idx] = (terms[idx].astype(F32) + hop[part - 1, q, g].astype(F32)).astype(BF16)
            scatter_first(part, r, what).start()

    def peer_half(r):
        q = quarter(r)
        peer_out[q] = half_terms(q, 1 - core).astype(BF16)
        peer_copy(q).start()

    def own_half(r):
        q = quarter(r)
        total = half_terms(q, core)
        peer_copy(q).wait_recv()
        total = (total + peer_in[q].astype(F32)).astype(BF16)
        for g in range(GROUPS):
            terms[g, q] = total[:, g * 128 : (g + 1) * 128].reshape(4, 4, 16, 128)

    def send_terms(r):
        if r == 0:
            for upper in (0, 1):
                hop_first(upper).start()
        for part in (1, 2):
            scatter_first(part, r, 0).start()
            scatter_first(part, r, 2 if r % 2 == 0 else 1).start()
            if r in DIRECT:
                scatter_first(part, r, 1 if r % 2 == 0 else 2).start()

    def combine_first(r):
        upper = r - 1
        hop_first(upper).wait_recv()
        for g in range(3):
            idx = (g, quarter(r), pl.ds(2 * upper, 2))
            terms[idx] = (terms[idx].astype(F32) + hop0[upper, g].astype(F32)).astype(BF16)
        slab_first(r).start()

    proj_steps(0, 2)
    blk_copy.wait_recv()
    theirs = blk_in[...]
    block16 = jnp.concatenate(
        [jnp.where(first, own_blk, theirs), jnp.where(first, theirs, own_blk)], axis=0
    ).astype(BF16)
    for g in range(GROUPS + 1):
        right[core, g, me[0], me[1], me[2]] = block16[:, g * 128 : (g + 1) * 128]
    for k, m in PLANE:
        for part in PARTS:
            scattered(part, k, m).start()

    proj_steps(2, 4)
    pltpu.make_async_copy(cot, cot, load_sem.at[0]).wait()
    peer_half(0)
    peer_half(1)
    own_half(0)
    send_terms(0)
    peer_half(2)
    own_half(1)
    send_terms(1)
    peer_half(3)
    for part in PARTS:
        settle(ag_send.at[part], ag_recv.at[part], 5, 3, 3).wait_recv()
    for part in PARTS:
        for k in (1, 3):
            neighbour(part, k).start()
    for part in PARTS:
        forward(part, 0, core).start()
    own_half(2)
    send_terms(2)
    own_half(3)
    send_terms(3)
    combine_first(1)
    combine(0)
    edge_load.wait()
    for i in range(OWN):
        u_acc[:, :, :, :, i * EDGE : (i + 1) * EDGE] = edge[i].astype(F32)

    def scatter(part, phase, k):
        axes = axes_of(part)
        groups = sum_groups(part)
        to = shifted(axes[phase], k)
        there = to[axes[phase]]
        if phase == 1:
            idx = [slice(None)] * 2
            idx[0 if axes[1] < axes[2] else 1] = there
            src, dst = sum1.at[groups, idx[0], idx[1]], slab2.at[k - 1, groups]
        else:
            src, dst = sum2.at[groups, there], slab3.at[k - 1, groups]
        return remote(
            src, dst, rs_send.at[part, phase - 1], rs_recv.at[part, phase - 1], device(to, core)
        )

    def settled(part, phase):
        send, recv = rs_send.at[part, phase - 1], rs_recv.at[part, phase - 1]
        return settle(send, recv, 9 if part < 2 else 6, 4 if phase == 1 else 1, 1)

    def scatter_add(part, phase):
        axes = axes_of(part)
        here = me[axes[phase]]
        first_group, count = 3 * part, 3 if part < 2 else GROUPS - 6
        if phase == 0:
            sem, tiles = ((2, (6, 4, 4)), (7, (6, 4, 4)), (8, (4, 4, 4)))[part]
            settle(r0_send.at[sem], r0_recv.at[sem], *tiles).wait_recv()
        else:
            settled(part, phase).wait_recv()
        for g in range(first_group, first_group + count):
            if phase == 0 and part > 0:
                for r in DIRECT:
                    q = quarter(r)
                    late = slab1[0, g, q].astype(F32) + hop[part - 1, q, g].astype(F32)
                    slab1[0, g, q] = late.astype(BF16)
            if phase == 0:
                idx = [slice(None)] * 3
                idx[axes[0]] = here
                total = terms[g, idx[0], idx[1], idx[2]].astype(F32)
                for k in range(2):
                    total += slab1[k, g].astype(F32)
                sum1[g] = total.astype(BF16)
            elif phase == 1:
                idx = [slice(None)] * 2
                idx[0 if axes[1] < axes[2] else 1] = here
                total = sum1[g, idx[0], idx[1]].astype(F32)
                for k in range(3):
                    total += slab2[k, g].astype(F32)
                sum2[g] = total.astype(BF16)
            else:
                total = sum2[g, here].astype(F32)
                for k in range(3):
                    total += slab3[k, g].astype(F32)
                fin_s[:, g * 128 : (g + 1) * 128] = total
        if phase < 2:
            for k in STEPS:
                scatter(part, phase + 1, k).start()

    def flat_plane(ref, lead, part, k):
        idx = plane_index(part, 2, shifted(axes_of(part)[2], (4 - k) % 4))
        return ref[lead + idx].reshape(256, ref.shape[-1])

    def count_of(part):
        return 3 if part < 2 else GROUPS - 6

    def left_plane(half, part, k):
        count = count_of(part)
        block = jnp.concatenate(
            [flat_plane(right, (half, 3 * part + n), part, k) for n in range(count)], axis=1
        )
        prod = lax.dot_general(
            block, flat_plane(cot, (), part, k), (((0,), (0,)), ((), ())), preferred_element_type=F32
        )
        rows = pl.ds(pl.multiple_of(half * HALF + part * 384, 128), count * 128)
        if k == 0:
            g_acc[rows, :] = prod
            return
        prod = prod + g_acc[rows, :]
        if k != 2:
            g_acc[rows, :] = prod
            return
        for n in range(count):
            gi = 3 * part + n
            for b in range(16):
                tile = prod[n * 128 + b * 8 : n * 128 + b * 8 + 8]
                lo = ((gi % 2) * 16 + b) * EDGE
                for m in range(OWN // 2):
                    pair = jnp.concatenate(
                        [tile[:, m * 256 : m * 256 + EDGE], tile[:, m * 256 + EDGE : m * 256 + 256]], axis=0
                    ).astype(BF16)
                    top = pl.multiple_of((half * 4 + gi // 2) * 64 + m * 16, 16)
                    gmat[pl.ds(top, 16), lo : lo + EDGE] = pair

    def pair_plane(part, k):
        count = count_of(part)
        lhs = jnp.concatenate(
            [flat_plane(right, (half, 3 * part + n), part, k) for half in range(2) for n in range(count)], axis=1
        )
        rhs = jnp.concatenate(
            [proj[half * HALF + part * 384 : half * HALF + part * 384 + count * 128, :] for half in range(2)], axis=0
        )
        u = jnp.dot(lhs, rhs, preferred_element_type=F32)
        idx = plane_index(part, 2, shifted(axes_of(part)[2], (4 - k) % 4))
        u_acc[idx] = u_acc[idx] + u.reshape(4, 4, 16, OWN * EDGE)

    def forwarded(k):
        settle(fw_send.at[FORWARD[k]], fw_recv.at[FORWARD[k]], 9, 4, 4).wait_recv()

    def left_own(k):
        for part in PARTS:
            left_plane(core, part, k)

    def left_other(k):
        for part in PARTS:
            left_plane(1 - core, part, k)

    def pair(k):
        for part in PARTS:
            pair_plane(part, k)

    def neighbours():
        for part in PARTS:
            settle(nb_send.at[part], nb_recv.at[part], 6, 4, 4).wait_recv()
            for k in (1, 3):
                opposite(part, int(k == 3)).start()
        for k in (1, 3):
            for part in PARTS:
                forward(part, k, core).start()

    def opposites():
        for part in PARTS:
            settle(op_send.at[part], op_recv.at[part], 3, 4, 4).wait_recv()
            for upper in (0, 1):
                forward(part, 2 + 2 * upper, core).start()

    def reduce(phase):
        if phase == 0:
            for r in DIRECT:
                settle(r0_send.at[3 + r], r0_recv.at[3 + r], 5, 4, 1).wait_recv()
        for part in PARTS:
            scatter_add(part, phase)

    def left_gradient():
        gl = nt(gmat[...], wflat[...])
        for h in range(8):
            for i in range(OWN):
                tile = gl[h * 64 + i * 8 : h * 64 + i * 8 + 8] * (pad_ref[i].astype(F32) * (1.0 / SEQS))
                grad_s[pl.ds(h * 64 + i, 8, stride=OWN), :] = tile
        gn_ref[...] = jnp.dot(grad_s[...].astype(BF16), w1t_ref[...], preferred_element_type=F32)

    left_own(0)
    combine(1)
    combine_first(2)
    forwarded(0)
    left_other(0)
    pair(0)
    neighbours()
    left_own(1)
    left_own(3)
    forwarded(1)
    left_other(1)
    reduce(0)
    forwarded(3)
    left_other(3)
    opposites()
    pair(1)
    left_own(2)
    reduce(1)
    pair(3)
    forwarded(2)
    left_other(2)
    pair(2)
    for half in range(2):
        labels[half] = right[half, GROUPS]
    reduce(2)
    fin = fin_s[...]
    fin_out[...] = jnp.where(first, fin[8:], fin[:8])
    fin_mine = jnp.where(first, fin[:8], fin[8:])
    fin_copy = remote(fin_out, fin_in, misc_send.at[1], misc_recv.at[1], sibling)
    fin_copy.start()
    left_gradient()

    fin_copy.wait_recv()
    fin_theirs = fin_in[...]
    lo_half = jnp.where(first, fin_mine, fin_theirs) * keep_one
    hi_half = jnp.where(first, fin_theirs, fin_mine) * keep_one
    spread_rows = []
    for h in range(8):
        src = lo_half if h < 4 else hi_half
        base = src[:, (h % 4) * 256 : (h % 4) * 256 + 256]
        spread_rows.append(jnp.where(mine, base[None], 0.0).reshape(8 * OWN, FEAT))
    gr = jnp.concatenate(spread_rows, axis=0).astype(BF16)
    gn_ref[...] += jnp.dot(gr, w2e, preferred_element_type=F32)

    blk_copy.wait_send()
    fin_copy.wait_send()
    for part in PARTS:
        for phase in (1, 2):
            settled(part, phase).wait_send()
        settle(ag_send.at[part], ag_recv.at[part], 5, 3, 3).wait_send()
        settle(nb_send.at[part], nb_recv.at[part], 6, 4, 4).wait_send()
        settle(op_send.at[part], op_recv.at[part], 3, 4, 4).wait_send()
    for k in range(4):
        settle(fw_send.at[k], fw_recv.at[k], 9, 4, 4).wait_send()
    for r in range(4):
        settle(r0_send.at[3 + r], r0_recv.at[3 + r], 5, 4, 1).wait_send()
        peer_copy(r).wait_send()
    for sem, tiles in ((2, (6, 4, 4)), (7, (6, 4, 4)), (8, (4, 4, 4))):
        settle(r0_send.at[sem], r0_recv.at[sem], *tiles).wait_send()
    for upper in (0, 1):
        hop_first(upper).wait_send()


def finish_kernel(
    u_ref, labels, gn_ref, unit_ref, rstd_ref, gain_ref, off_ref, smo_ref, pad_ref, mol_ref,
    pair_out, grad_out, held, grad, sems,
):
    def store(q):
        rows = pl.ds(q * 256, 256)
        return pltpu.make_async_copy(held.at[:, rows], pair_out.at[:, rows], sems.at[q])

    grad_store = pltpu.make_async_copy(grad, grad_out, sems.at[4])

    def pair(q):
        for lo in range(q * 256, q * 256 + 256, 64):
            rows = slice(lo, lo + 64)
            keep_j = labels[0, rows, :].astype(F32)
            mol_j = labels[1, rows, :].astype(F32)
            apart = keep_j * off_ref[...]
            together = keep_j * (off_ref[...] + smo_ref[...])
            for i in range(OWN):
                extra = jnp.where(mol_j == mol_ref[i].astype(F32), together, apart) * pad_ref[i].astype(F32)
                held[i, rows, :] = (u_ref[rows, i * EDGE : (i + 1) * EDGE] + extra).astype(BF16)
        store(q).start()

    pair(0)
    pair(1)
    unit = unit_ref[...]
    gained = gn_ref[...] * gain_ref[...]
    result = rstd_ref[:, :1] * (
        gained
        - jnp.mean(gained, axis=-1, keepdims=True)
        - unit * jnp.mean(gained * unit, axis=-1, keepdims=True)
    )
    grad[...] = result.reshape(SEQS, OWN, FEAT)
    grad_store.start()
    pair(2)
    pair(3)
    for q in range(4):
        store(q).wait()
    grad_store.wait()


def local(x, gain, w1, w2, wf, off, smo, edge, cot, pad, mol):
    vmem = pl.BlockSpec(memory_space=pltpu.VMEM)
    smem = pl.BlockSpec(memory_space=pltpu.SMEM)
    hbm = pl.BlockSpec(memory_space=pl.ANY)
    dma = pltpu.SemaphoreType.DMA
    gain = gain.reshape(1, FEAT)
    operands = (x, gain, w1.T, w2.T, wf) + tuple(
        v.reshape(OWN, 4, 4, 4, 16, EDGE) for v in (edge, cot)
    ) + (pad, mol)
    u, labels, gn, unit, rstd = pl.pallas_call(
        exchange_kernel,
        out_shape=(
            pltpu.VMEM((4, 4, 4, 16, OWN * EDGE), F32),
            pltpu.VMEM((2, 4, 4, 4, 16, 128), BF16),
            pltpu.VMEM((SEQS * OWN, FEAT), F32),
            pltpu.VMEM((SEQS * OWN, FEAT), F32),
            pltpu.VMEM((SEQS * OWN, 128), F32),
        ),
        in_specs=[hbm] * 9,
        out_specs=(vmem,) * 5,
        scratch_shapes=[
            pltpu.VMEM((SEQS, OWN, FEAT), BF16),
            pltpu.VMEM((1, FEAT), F32),
            pltpu.VMEM((FACTOR, FEAT), BF16),
            pltpu.VMEM((FACTOR, FEAT), BF16),
            pltpu.VMEM((FACTOR * FACTOR, EDGE), BF16),
            pltpu.SMEM((OWN,), jnp.int32),
            pltpu.SMEM((OWN,), jnp.int32),
            pltpu.VMEM((OWN, 4, 4, 4, 16, EDGE), BF16),
            pltpu.VMEM((4, 4, 4, 16, OWN * EDGE), BF16),
            pltpu.VMEM((2, GROUPS + 1, 4, 4, 4, 16, 128), BF16),
            pltpu.VMEM((SEQS * OWN, FACTOR), BF16),
            pltpu.VMEM((2 * HALF, OWN * EDGE), BF16),
            pltpu.VMEM((GROUPS, 4, 4, 4, 16, 128), BF16),
            pltpu.VMEM((4, 256, HALF), BF16),
            pltpu.VMEM((4, 256, HALF), BF16),
            pltpu.VMEM((2, 3, 2, 4, 16, 128), BF16),
            pltpu.VMEM((2, 4, GROUPS, 4, 16, 128), BF16),
            pltpu.VMEM((2, GROUPS, 4, 4, 16, 128), BF16),
            pltpu.VMEM((GROUPS, 4, 4, 16, 128), BF16),
            pltpu.VMEM((3, GROUPS, 4, 16, 128), BF16),
            pltpu.VMEM((GROUPS, 4, 16, 128), BF16),
            pltpu.VMEM((3, GROUPS, 16, 128), BF16),
            pltpu.VMEM((2 * HALF, OWN * EDGE), F32),
            pltpu.VMEM((SEQS * OWN, FACTOR * EDGE), BF16),
            pltpu.VMEM((FACTOR * FACTOR, EDGE), F32),
            pltpu.VMEM((FACTOR, FACTOR * EDGE), BF16),
            pltpu.VMEM((SEQS * OWN, FACTOR), F32),
            pltpu.VMEM((SEQS * OWN, FACTOR), F32),
            pltpu.VMEM((OWN, HALF + 128), F32),
            pltpu.VMEM((OWN, HALF + 128), F32),
            pltpu.VMEM((16, HALF), F32),
            pltpu.VMEM((OWN, HALF), F32),
            pltpu.VMEM((OWN, HALF), F32),
            dma((9,)),
            dma((3,)),
            dma((3,)),
            dma((3,)),
            dma((3,)),
            dma((3,)),
            dma((3,)),
            dma((4,)),
            dma((4,)),
            dma((9,)),
            dma((9,)),
            dma((3, 2)),
            dma((3, 2)),
            dma((4,)),
            dma((4,)),
            dma((2,)),
            dma((2,)),
        ],
        compiler_params=pltpu.CompilerParams(
            collective_id=0, has_side_effects=True, vmem_limit_bytes=50 * 2**20
        ),
        name="outer_product_mean",
    )(*(pltpu.with_memory_space_constraint(v, pltpu.HBM) for v in operands))
    return pl.pallas_call(
        finish_kernel,
        out_shape=(
            jax.ShapeDtypeStruct(edge.shape, BF16),
            jax.ShapeDtypeStruct(x.shape, F32),
        ),
        in_specs=[vmem] * 8 + [smem, smem],
        out_specs=(hbm, hbm),
        scratch_shapes=[
            pltpu.VMEM((OWN, LENGTH, EDGE), BF16),
            pltpu.VMEM((SEQS, OWN, FEAT), F32),
            dma((5,)),
        ],
        compiler_params=pltpu.CompilerParams(vmem_limit_bytes=16 * 2**20),
        name="finish",
    )(
        u.reshape(LENGTH, OWN * EDGE), labels.reshape(2, LENGTH, 128), gn, unit, rstd, gain,
        off.reshape(1, EDGE), smo.reshape(1, EDGE), pad, mol,
    )


def solution(mesh):
    rows = ("branch", "res")
    return jax.shard_map(
        local,
        mesh=mesh,
        in_specs=(
            P(None, rows, None), P(), P(), P(), P(), P(), P(),
            P(rows, None, None), P(rows, None, None), P(rows), P(rows),
        ),
        out_specs=(P(rows, None, None), P(None, rows, None)),
        check_vma=False,
    )
```

```python
import jax
import jax.numpy as jnp
from jax import lax
from jax.experimental import pallas as pl
from jax.experimental.pallas import tpu as pltpu
from jax.sharding import PartitionSpec as P

MESH = pl.DeviceIdType.MESH
F32 = jnp.float32
BF16 = jnp.bfloat16

SEQS = 64
FEAT = 256
FACTOR = 32
EDGE = 128
LENGTH = 1024
OWN = 8
HALF = 1024
GROUPS = HALF // 128
EPSILON = 1e-05

PARTS = (0, 1, 2)
STEPS = (1, 2, 3)
FORWARD = (0, 1, 3, 2, 3)
DIRECT = (2, 3)
PLANE = tuple((k, m) for k in range(4) for m in range(4) if k or m)


def axes_of(part):
    return (part % 3, (part + 1) % 3, (part + 2) % 3)


def sum_groups(part):
    return pl.ds(3 * part, 3 if part < 2 else GROUPS - 6)


def nt(a, b):
    return lax.dot_general(a, b, (((1,), (1,)), ((), ())), preferred_element_type=F32)


def normalise(x):
    xs = x.astype(F32).reshape(SEQS * OWN, FEAT)
    centred = xs - jnp.mean(xs, axis=-1, keepdims=True)
    rstd = lax.rsqrt(jnp.mean(centred * centred, axis=-1, keepdims=True) + EPSILON)
    return centred * rstd, rstd


def exchange_kernel(
    x_hbm, gain_hbm, w1t_hbm, w2t_hbm, wf_hbm, edge_hbm, cot_hbm, pad_hbm, mol_hbm,
    u_acc, labels, gn_ref, unit_ref, rstd_ref,
    x_ref, gain_ref, w1t_ref, w2t_ref, wf_ref, pad_ref, mol_ref,
    edge, cot, right, left_b, proj, terms, peer_out, peer_in, hop0, hop, slab1, sum1, slab2, sum2, slab3,
    g_acc, gmat, wff, wflat, left_s, grad_s, blk_out, blk_in, fin_s, fin_out, fin_in,
    load_sem,
    ag_send, ag_recv, nb_send, nb_recv, op_send, op_recv, fw_send, fw_recv,
    r0_send, r0_recv, rs_send, rs_recv, pr_send, pr_recv, misc_send, misc_recv,
):
    branch, res = lax.axis_index("branch"), lax.axis_index("res")
    core = res % 2
    first = core == 0
    me = (branch * 2 + res // 32, (res // 8) % 4, (res // 2) % 4)

    def device(at, c):
        return (at[0] // 2, (at[0] % 2) * 32 + at[1] * 8 + at[2] * 2 + c)

    def shifted(axis, k, other=None, m=0):
        at = list(me)
        at[axis] = (at[axis] + k) % 4
        if other is not None:
            at[other] = (at[other] + m) % 4
        return at

    def remote(src, dst, send, recv, to):
        return pltpu.make_async_remote_copy(src, dst, send, recv, device_id=to, device_id_type=MESH)

    sibling = device(me, 1 - core)

    def settle(send, recv, groups, rows, cols):
        block = right.at[0, pl.ds(0, groups), pl.ds(0, rows), pl.ds(0, cols), 0]
        return remote(block, block, send, recv, sibling)

    small = (
        (x_hbm, x_ref), (gain_hbm, gain_ref), (w2t_hbm, w2t_ref), (w1t_hbm, w1t_ref),
        (wf_hbm, wf_ref), (pad_hbm, pad_ref), (mol_hbm, mol_ref),
    )
    small_loads = [
        pltpu.make_async_copy(src, dst, load_sem.at[2 + n]) for n, (src, dst) in enumerate(small)
    ]
    for cp in small_loads:
        cp.start()

    barrier = pltpu.get_barrier_semaphore()
    for part in PARTS:
        axes = axes_of(part)
        for k in STEPS:
            for m in range(4):
                to = device(shifted(axes[0], k, axes[1], m), core)
                pl.semaphore_signal(barrier, inc=1, device_id=to, device_id_type=MESH)
    pl.semaphore_signal(barrier, inc=1, device_id=sibling, device_id_type=MESH)

    cot_loads = [
        pltpu.make_async_copy(cot_hbm.at[i], cot.at[:, :, :, :, pl.ds(i * EDGE, EDGE)], load_sem.at[0])
        for i in range(OWN)
    ]
    edge_load = pltpu.make_async_copy(edge_hbm, edge, load_sem.at[1])
    for cp in cot_loads:
        cp.start()
    edge_load.start()

    for cp in small_loads:
        cp.wait()
    unit, rstd = normalise(x_ref[...])
    unit_ref[...] = unit
    rstd_ref[...] = jnp.broadcast_to(rstd, rstd_ref.shape)
    normed = (unit * gain_ref[...]).astype(BF16)

    lane = lax.broadcasted_iota(jnp.int32, (FACTOR, FEAT), 1)
    row = lax.broadcasted_iota(jnp.int32, (FACTOR, FEAT), 0)
    spread = jnp.where(lane // 8 == row, 1.0, 0.0).astype(BF16)
    w2e = lax.dot_general(
        spread, w2t_ref[...], (((0,), (0,)), ((), ())), preferred_element_type=F32
    ).astype(BF16)

    rows8 = lax.broadcasted_iota(jnp.int32, (OWN, 128), 0)
    keep_col = jnp.zeros((OWN, 128), F32)
    mol_col = jnp.zeros((OWN, 128), F32)
    for i in range(OWN):
        keep_col = jnp.where(rows8 == i, pad_ref[i].astype(F32), keep_col)
        mol_col = jnp.where(rows8 == i, mol_ref[i].astype(F32), mol_col)
    keep_one = keep_col[:, :1]

    lane4 = lax.broadcasted_iota(jnp.int32, (8, OWN, FEAT), 2) % 8
    slot4 = lax.broadcasted_iota(jnp.int32, (8, OWN, FEAT), 0)
    mine = lane4 == slot4
    right_e = nt(normed, w2e).astype(BF16).astype(F32).reshape(8, 8, OWN, FEAT)
    flat = [jnp.sum(jnp.where(mine, right_e[h], 0.0), axis=0) * keep_one for h in range(8)]
    half0 = jnp.concatenate(flat[:4] + [keep_col], axis=1)
    half1 = jnp.concatenate(flat[4:] + [mol_col], axis=1)
    blk_out[...] = jnp.where(first, half1, half0)
    own_blk = jnp.where(first, half0, half1)

    left_s[...] = nt(normed, w1t_ref[...]).astype(BF16).astype(F32)
    wff[...] = wf_ref[...].astype(F32)
    for b in range(FACTOR):
        wflat[:, b * EDGE : (b + 1) * EDGE] = wff[pl.ds(b, FACTOR, stride=FACTOR), :].astype(BF16)
    for i in range(OWN):
        rows = left_s[pl.ds(i, SEQS, stride=OWN), :] * (pad_ref[i].astype(F32) * (1.0 / SEQS))
        left_b[i * SEQS : (i + 1) * SEQS, :] = rows.astype(BF16)

    def proj_steps(start, stop):
        left = left_b[...]

        def step(m, carry):
            for v in range(4):
                n = m * 4 + v
                y = jnp.dot(left, wflat[:, pl.ds(pl.multiple_of(n * 256, 256), 256)], preferred_element_type=F32)
                for i in range(OWN):
                    for h in range(8):
                        tile = y[i * SEQS + h * 8 : i * SEQS + h * 8 + 8]
                        pair = jnp.concatenate([tile[:, :EDGE], tile[:, EDGE:]], axis=0).astype(BF16)
                        top = pl.multiple_of(h * 256 + n * 16, 16)
                        proj[pl.ds(top, 16), i * EDGE : (i + 1) * EDGE] = pair
            return carry

        lax.fori_loop(start, stop, step, 0)

    pl.semaphore_wait(barrier, 37)
    blk_copy = remote(blk_out, blk_in, misc_send.at[0], misc_recv.at[0], sibling)
    blk_copy.start()

    def plane_index(part, phase, at):
        idx = list(at)
        for axis in axes_of(part)[:phase]:
            idx[axis] = slice(None)
        return tuple(idx)

    def block_ref(half, part, phase, at):
        return right.at[(half, pl.ds(3 * part, 3)) + plane_index(part, phase, at)]

    def half_ref(half, part, at, upper):
        idx = list(plane_index(part, 2, at))
        idx[axes_of(part)[0]] = pl.ds(2 * upper, 2)
        return right.at[(half, pl.ds(3 * part, 3)) + tuple(idx)]

    def scattered(part, k, m, receive=False):
        axes = axes_of(part)
        there = shifted(axes[0], (4 - k) % 4, axes[1], (4 - m) % 4)
        block = block_ref(core, part, 0, there if receive else me)
        to = device(there if receive else shifted(axes[0], k, axes[1], m), core)
        return remote(block, block, ag_send.at[part], ag_recv.at[part], to)

    def neighbour(part, k, receive=False):
        axis = axes_of(part)[2]
        at = shifted(axis, 4 - k) if receive else me
        block = block_ref(core, part, 2, at)
        to = device(shifted(axis, 4 - k if receive else k), core)
        return remote(block, block, nb_send.at[part], nb_recv.at[part], to)

    def opposite(part, upper, receive=False):
        axis = axes_of(part)[2]
        k = 3 if upper else 1
        at = shifted(axis, 2) if receive else shifted(axis, 4 - k)
        block = half_ref(core, part, at, upper)
        to = device(shifted(axis, 4 - k if receive else k), core)
        return remote(block, block, op_send.at[part], op_recv.at[part], to)

    def forward(part, k, half):
        if k in (2, 4):
            block = half_ref(half, part, shifted(axes_of(part)[2], 2), int(k == 4))
        else:
            block = block_ref(half, part, 2, shifted(axes_of(part)[2], 4 - k))
        return remote(block, block, fw_send.at[FORWARD[k]], fw_recv.at[FORWARD[k]], sibling)

    def peer_copy(q):
        return remote(peer_out.at[q], peer_in.at[q], pr_send.at[q], pr_recv.at[q], sibling)

    def half_terms(q, half):
        rows = cot[q].reshape(256, OWN * EDGE)
        return nt(rows, proj[pl.ds(pl.multiple_of(half * HALF, HALF), HALF), :])

    def quarter(r):
        return (me[0] + (2, 1, 3, 0)[r]) % 4

    def hop_first(upper):
        groups = sum_groups(0)
        return remote(
            terms.at[groups, quarter(0), pl.ds(2 * upper, 2)], hop0.at[upper, groups],
            r0_send.at[upper], r0_recv.at[upper], device(shifted(0, 3 if upper else 1), core),
        )

    def slab_first(r):
        groups = sum_groups(0)
        return remote(
            terms.at[groups, quarter(r)], slab1.at[r - 1, groups],
            r0_send.at[2], r0_recv.at[2], device(shifted(0, 1 if r == 1 else 3), core),
        )

    def scatter_first(part, r, what):
        groups, q = sum_groups(part), quarter(r)
        up = r % 2 == 0 if what == 0 else what == 1
        there = shifted(part, 2 if what == 0 else (1 if up else 3))
        if part == 1:
            src = terms.at[groups, q, there[1]]
        else:
            src = terms.at[groups, q, :, there[2]]
        dst = hop.at[part - 1, q, groups] if what == 0 else slab1.at[what - 1, groups, q]
        sem = 3 + r if what == 0 else 6 + part
        return remote(
            src, dst, r0_send.at[sem], r0_recv.at[sem],
            device(there if what == 0 and r in DIRECT else shifted(part, 1 if up else 3), core),
        )

    def combine(r):
        q = quarter(r)
        what = 1 if r % 2 == 0 else 2
        settle(r0_send.at[3 + r], r0_recv.at[3 + r], 5, 4, 1).wait_recv()
        for part in (1, 2):
            there = shifted(part, 1 if what == 1 else 3)
            for g in range(3 * part, 3 * part + (3 if part < 2 else GROUPS - 6)):
                idx = (g, q, there[1]) if part == 1 else (g, q, slice(None), there[2])
                terms[idx] = (terms[idx].astype(F32) + hop[part - 1, q, g].astype(F32)).astype(BF16)
            scatter_first(part, r, what).start()

    def peer_half(r):
        q = quarter(r)
        peer_out[q] = half_terms(q, 1 - core).astype(BF16)
        peer_copy(q).start()

    def own_half(r):
        q = quarter(r)
        total = half_terms(q, core)
        peer_copy(q).wait_recv()
        total = (total + peer_in[q].astype(F32)).astype(BF16)
        for g in range(GROUPS):
            terms[g, q] = total[:, g * 128 : (g + 1) * 128].reshape(4, 4, 16, 128)

    def send_terms(r):
        if r == 0:
            for upper in (0, 1):
                hop_first(upper).start()
        for part in (1, 2):
            scatter_first(part, r, 0).start()
            scatter_first(part, r, 2 if r % 2 == 0 else 1).start()
            if r in DIRECT:
                scatter_first(part, r, 1 if r % 2 == 0 else 2).start()

    def combine_first(r):
        upper = r - 1
        hop_first(upper).wait_recv()
        for g in range(3):
            idx = (g, quarter(r), pl.ds(2 * upper, 2))
            terms[idx] = (terms[idx].astype(F32) + hop0[upper, g].astype(F32)).astype(BF16)
        slab_first(r).start()

    proj_steps(0, 2)
    blk_copy.wait_recv()
    theirs = blk_in[...]
    block16 = jnp.concatenate(
        [jnp.where(first, own_blk, theirs), jnp.where(first, theirs, own_blk)], axis=0
    ).astype(BF16)
    for g in range(GROUPS + 1):
        right[core, g, me[0], me[1], me[2]] = block16[:, g * 128 : (g + 1) * 128]
    for k, m in PLANE:
        for part in PARTS:
            scattered(part, k, m).start()

    proj_steps(2, 4)
    pltpu.make_async_copy(cot, cot, load_sem.at[0]).wait()
    peer_half(0)
    peer_half(1)
    peer_half(2)
    own_half(0)
    send_terms(0)
    own_half(1)
    send_terms(1)
    peer_half(3)
    own_half(2)
    send_terms(2)
    for part in PARTS:
        settle(ag_send.at[part], ag_recv.at[part], 5, 3, 3).wait_recv()
    for part in PARTS:
        for k in (1, 3):
            neighbour(part, k).start()
    for part in PARTS:
        forward(part, 0, core).start()
    own_half(3)
    send_terms(3)
    combine_first(1)
    combine(0)
    edge_load.wait()
    for i in range(OWN):
        u_acc[:, :, :, :, i * EDGE : (i + 1) * EDGE] = edge[i].astype(F32)

    def scatter(part, phase, k):
        axes = axes_of(part)
        groups = sum_groups(part)
        to = shifted(axes[phase], k)
        there = to[axes[phase]]
        if phase == 1:
            idx = [slice(None)] * 2
            idx[0 if axes[1] < axes[2] else 1] = there
            src, dst = sum1.at[groups, idx[0], idx[1]], slab2.at[k - 1, groups]
        else:
            src, dst = sum2.at[groups, there], slab3.at[k - 1, groups]
        return remote(
            src, dst, rs_send.at[part, phase - 1], rs_recv.at[part, phase - 1], device(to, core)
        )

    def settled(part, phase):
        send, recv = rs_send.at[part, phase - 1], rs_recv.at[part, phase - 1]
        return settle(send, recv, 9 if part < 2 else 6, 4 if phase == 1 else 1, 1)

    def scatter_add(part, phase):
        axes = axes_of(part)
        here = me[axes[phase]]
        first_group, count = 3 * part, 3 if part < 2 else GROUPS - 6
        if phase == 0:
            sem, tiles = ((2, (6, 4, 4)), (7, (6, 4, 4)), (8, (4, 4, 4)))[part]
            settle(r0_send.at[sem], r0_recv.at[sem], *tiles).wait_recv()
        else:
            settled(part, phase).wait_recv()
        for g in range(first_group, first_group + count):
            if phase == 0 and part > 0:
                for r in DIRECT:
                    q = quarter(r)
                    late = slab1[0, g, q].astype(F32) + hop[part - 1, q, g].astype(F32)
                    slab1[0, g, q] = late.astype(BF16)
            if phase == 0:
                idx = [slice(None)] * 3
                idx[axes[0]] = here
                total = terms[g, idx[0], idx[1], idx[2]].astype(F32)
                for k in range(2):
                    total += slab1[k, g].astype(F32)
                sum1[g] = total.astype(BF16)
            elif phase == 1:
                idx = [slice(None)] * 2
                idx[0 if axes[1] < axes[2] else 1] = here
                total = sum1[g, idx[0], idx[1]].astype(F32)
                for k in range(3):
                    total += slab2[k, g].astype(F32)
                sum2[g] = total.astype(BF16)
            else:
                total = sum2[g, here].astype(F32)
                for k in range(3):
                    total += slab3[k, g].astype(F32)
                fin_s[:, g * 128 : (g + 1) * 128] = total
        if phase < 2:
            for k in STEPS:
                scatter(part, phase + 1, k).start()

    def flat_plane(ref, lead, part, k):
        idx = plane_index(part, 2, shifted(axes_of(part)[2], (4 - k) % 4))
        return ref[lead + idx].reshape(256, ref.shape[-1])

    def count_of(part):
        return 3 if part < 2 else GROUPS - 6

    def left_plane(half, part, k):
        count = count_of(part)
        block = jnp.concatenate(
            [flat_plane(right, (half, 3 * part + n), part, k) for n in range(count)], axis=1
        )
        prod = lax.dot_general(
            block, flat_plane(cot, (), part, k), (((0,), (0,)), ((), ())), preferred_element_type=F32
        )
        rows = pl.ds(pl.multiple_of(half * HALF + part * 384, 128), count * 128)
        if k == 0:
            g_acc[rows, :] = prod
            return
        prod = prod + g_acc[rows, :]
        if k != 2:
            g_acc[rows, :] = prod
            return
        for n in range(count):
            gi = 3 * part + n
            for b in range(16):
                tile = prod[n * 128 + b * 8 : n * 128 + b * 8 + 8]
                lo = ((gi % 2) * 16 + b) * EDGE
                for m in range(OWN // 2):
                    pair = jnp.concatenate(
                        [tile[:, m * 256 : m * 256 + EDGE], tile[:, m * 256 + EDGE : m * 256 + 256]], axis=0
                    ).astype(BF16)
                    top = pl.multiple_of((half * 4 + gi // 2) * 64 + m * 16, 16)
                    gmat[pl.ds(top, 16), lo : lo + EDGE] = pair

    def pair_plane(part, k):
        count = count_of(part)
        lhs = jnp.concatenate(
            [flat_plane(right, (half, 3 * part + n), part, k) for half in range(2) for n in range(count)], axis=1
        )
        rhs = jnp.concatenate(
            [proj[half * HALF + part * 384 : half * HALF + part * 384 + count * 128, :] for half in range(2)], axis=0
        )
        u = jnp.dot(lhs, rhs, preferred_element_type=F32)
        idx = plane_index(part, 2, shifted(axes_of(part)[2], (4 - k) % 4))
        u_acc[idx] = u_acc[idx] + u.reshape(4, 4, 16, OWN * EDGE)

    def forwarded(k):
        settle(fw_send.at[FORWARD[k]], fw_recv.at[FORWARD[k]], 9, 4, 4).wait_recv()

    def left_own(k):
        for part in PARTS:
            left_plane(core, part, k)

    def left_other(k):
        for part in PARTS:
            left_plane(1 - core, part, k)

    def pair(k):
        for part in PARTS:
            pair_plane(part, k)

    def neighbours():
        for part in PARTS:
            settle(nb_send.at[part], nb_recv.at[part], 6, 4, 4).wait_recv()
            for k in (1, 3):
                opposite(part, int(k == 3)).start()
        for k in (1, 3):
            for part in PARTS:
                forward(part, k, core).start()

    def opposites():
        for part in PARTS:
            settle(op_send.at[part], op_recv.at[part], 3, 4, 4).wait_recv()
            for upper in (0, 1):
                forward(part, 2 + 2 * upper, core).start()

    def reduce(phase):
        if phase == 0:
            for r in DIRECT:
                settle(r0_send.at[3 + r], r0_recv.at[3 + r], 5, 4, 1).wait_recv()
        for part in PARTS:
            scatter_add(part, phase)

    def left_gradient():
        gl = nt(gmat[...], wflat[...])
        for h in range(8):
            for i in range(OWN):
                tile = gl[h * 64 + i * 8 : h * 64 + i * 8 + 8] * (pad_ref[i].astype(F32) * (1.0 / SEQS))
                grad_s[pl.ds(h * 64 + i, 8, stride=OWN), :] = tile
        gn_ref[...] = jnp.dot(grad_s[...].astype(BF16), w1t_ref[...], preferred_element_type=F32)

    left_own(0)
    combine(1)
    combine_first(2)
    forwarded(0)
    left_other(0)
    pair(0)
    neighbours()
    left_own(1)
    left_own(3)
    forwarded(1)
    left_other(1)
    reduce(0)
    forwarded(3)
    left_other(3)
    opposites()
    pair(1)
    left_own(2)
    reduce(1)
    pair(3)
    forwarded(2)
    left_other(2)
    pair(2)
    for half in range(2):
        labels[half] = right[half, GROUPS]
    reduce(2)
    fin = fin_s[...]
    fin_out[...] = jnp.where(first, fin[8:], fin[:8])
    fin_mine = jnp.where(first, fin[:8], fin[8:])
    fin_copy = remote(fin_out, fin_in, misc_send.at[1], misc_recv.at[1], sibling)
    fin_copy.start()
    left_gradient()

    fin_copy.wait_recv()
    fin_theirs = fin_in[...]
    lo_half = jnp.where(first, fin_mine, fin_theirs) * keep_one
    hi_half = jnp.where(first, fin_theirs, fin_mine) * keep_one
    spread_rows = []
    for h in range(8):
        src = lo_half if h < 4 else hi_half
        base = src[:, (h % 4) * 256 : (h % 4) * 256 + 256]
        spread_rows.append(jnp.where(mine, base[None], 0.0).reshape(8 * OWN, FEAT))
    gr = jnp.concatenate(spread_rows, axis=0).astype(BF16)
    gn_ref[...] += jnp.dot(gr, w2e, preferred_element_type=F32)

    blk_copy.wait_send()
    fin_copy.wait_send()
    for part in PARTS:
        for phase in (1, 2):
            settled(part, phase).wait_send()
        settle(ag_send.at[part], ag_recv.at[part], 5, 3, 3).wait_send()
        settle(nb_send.at[part], nb_recv.at[part], 6, 4, 4).wait_send()
        settle(op_send.at[part], op_recv.at[part], 3, 4, 4).wait_send()
    for k in range(4):
        settle(fw_send.at[k], fw_recv.at[k], 9, 4, 4).wait_send()
    for r in range(4):
        settle(r0_send.at[3 + r], r0_recv.at[3 + r], 5, 4, 1).wait_send()
        peer_copy(r).wait_send()
    for sem, tiles in ((2, (6, 4, 4)), (7, (6, 4, 4)), (8, (4, 4, 4))):
        settle(r0_send.at[sem], r0_recv.at[sem], *tiles).wait_send()
    for upper in (0, 1):
        hop_first(upper).wait_send()


def finish_kernel(
    u_ref, labels, gn_ref, unit_ref, rstd_ref, gain_ref, off_ref, smo_ref, pad_ref, mol_ref,
    pair_out, grad_out, held, grad, sems,
):
    def store(q):
        rows = pl.ds(q * 256, 256)
        return pltpu.make_async_copy(held.at[:, rows], pair_out.at[:, rows], sems.at[q])

    grad_store = pltpu.make_async_copy(grad, grad_out, sems.at[4])

    def pair(q):
        for lo in range(q * 256, q * 256 + 256, 64):
            rows = slice(lo, lo + 64)
            keep_j = labels[0, rows, :].astype(F32)
            mol_j = labels[1, rows, :].astype(F32)
            apart = keep_j * off_ref[...]
            together = keep_j * (off_ref[...] + smo_ref[...])
            for i in range(OWN):
                extra = jnp.where(mol_j == mol_ref[i].astype(F32), together, apart) * pad_ref[i].astype(F32)
                held[i, rows, :] = (u_ref[rows, i * EDGE : (i + 1) * EDGE] + extra).astype(BF16)
        store(q).start()

    pair(0)
    pair(1)
    unit = unit_ref[...]
    gained = gn_ref[...] * gain_ref[...]
    result = rstd_ref[:, :1] * (
        gained
        - jnp.mean(gained, axis=-1, keepdims=True)
        - unit * jnp.mean(gained * unit, axis=-1, keepdims=True)
    )
    grad[...] = result.reshape(SEQS, OWN, FEAT)
    grad_store.start()
    pair(2)
    pair(3)
    for q in range(4):
        store(q).wait()
    grad_store.wait()


def local(x, gain, w1, w2, wf, off, smo, edge, cot, pad, mol):
    vmem = pl.BlockSpec(memory_space=pltpu.VMEM)
    smem = pl.BlockSpec(memory_space=pltpu.SMEM)
    hbm = pl.BlockSpec(memory_space=pl.ANY)
    dma = pltpu.SemaphoreType.DMA
    gain = gain.reshape(1, FEAT)
    operands = (x, gain, w1.T, w2.T, wf) + tuple(
        v.reshape(OWN, 4, 4, 4, 16, EDGE) for v in (edge, cot)
    ) + (pad, mol)
    u, labels, gn, unit, rstd = pl.pallas_call(
        exchange_kernel,
        out_shape=(
            pltpu.VMEM((4, 4, 4, 16, OWN * EDGE), F32),
            pltpu.VMEM((2, 4, 4, 4, 16, 128), BF16),
            pltpu.VMEM((SEQS * OWN, FEAT), F32),
            pltpu.VMEM((SEQS * OWN, FEAT), F32),
            pltpu.VMEM((SEQS * OWN, 128), F32),
        ),
        in_specs=[hbm] * 9,
        out_specs=(vmem,) * 5,
        scratch_shapes=[
            pltpu.VMEM((SEQS, OWN, FEAT), BF16),
            pltpu.VMEM((1, FEAT), F32),
            pltpu.VMEM((FACTOR, FEAT), BF16),
            pltpu.VMEM((FACTOR, FEAT), BF16),
            pltpu.VMEM((FACTOR * FACTOR, EDGE), BF16),
            pltpu.SMEM((OWN,), jnp.int32),
            pltpu.SMEM((OWN,), jnp.int32),
            pltpu.VMEM((OWN, 4, 4, 4, 16, EDGE), BF16),
            pltpu.VMEM((4, 4, 4, 16, OWN * EDGE), BF16),
            pltpu.VMEM((2, GROUPS + 1, 4, 4, 4, 16, 128), BF16),
            pltpu.VMEM((SEQS * OWN, FACTOR), BF16),
            pltpu.VMEM((2 * HALF, OWN * EDGE), BF16),
            pltpu.VMEM((GROUPS, 4, 4, 4, 16, 128), BF16),
            pltpu.VMEM((4, 256, HALF), BF16),
            pltpu.VMEM((4, 256, HALF), BF16),
            pltpu.VMEM((2, 3, 2, 4, 16, 128), BF16),
            pltpu.VMEM((2, 4, GROUPS, 4, 16, 128), BF16),
            pltpu.VMEM((2, GROUPS, 4, 4, 16, 128), BF16),
            pltpu.VMEM((GROUPS, 4, 4, 16, 128), BF16),
            pltpu.VMEM((3, GROUPS, 4, 16, 128), BF16),
            pltpu.VMEM((GROUPS, 4, 16, 128), BF16),
            pltpu.VMEM((3, GROUPS, 16, 128), BF16),
            pltpu.VMEM((2 * HALF, OWN * EDGE), F32),
            pltpu.VMEM((SEQS * OWN, FACTOR * EDGE), BF16),
            pltpu.VMEM((FACTOR * FACTOR, EDGE), F32),
            pltpu.VMEM((FACTOR, FACTOR * EDGE), BF16),
            pltpu.VMEM((SEQS * OWN, FACTOR), F32),
            pltpu.VMEM((SEQS * OWN, FACTOR), F32),
            pltpu.VMEM((OWN, HALF + 128), F32),
            pltpu.VMEM((OWN, HALF + 128), F32),
            pltpu.VMEM((16, HALF), F32),
            pltpu.VMEM((OWN, HALF), F32),
            pltpu.VMEM((OWN, HALF), F32),
            dma((9,)),
            dma((3,)),
            dma((3,)),
            dma((3,)),
            dma((3,)),
            dma((3,)),
            dma((3,)),
            dma((4,)),
            dma((4,)),
            dma((9,)),
            dma((9,)),
            dma((3, 2)),
            dma((3, 2)),
            dma((4,)),
            dma((4,)),
            dma((2,)),
            dma((2,)),
        ],
        compiler_params=pltpu.CompilerParams(
            collective_id=0, has_side_effects=True, vmem_limit_bytes=50 * 2**20
        ),
        name="outer_product_mean",
    )(*(pltpu.with_memory_space_constraint(v, pltpu.HBM) for v in operands))
    return pl.pallas_call(
        finish_kernel,
        out_shape=(
            jax.ShapeDtypeStruct(edge.shape, BF16),
            jax.ShapeDtypeStruct(x.shape, F32),
        ),
        in_specs=[vmem] * 8 + [smem, smem],
        out_specs=(hbm, hbm),
        scratch_shapes=[
            pltpu.VMEM((OWN, LENGTH, EDGE), BF16),
            pltpu.VMEM((SEQS, OWN, FEAT), F32),
            dma((5,)),
        ],
        compiler_params=pltpu.CompilerParams(vmem_limit_bytes=16 * 2**20),
        name="finish",
    )(
        u.reshape(LENGTH, OWN * EDGE), labels.reshape(2, LENGTH, 128), gn, unit, rstd, gain,
        off.reshape(1, EDGE), smo.reshape(1, EDGE), pad, mol,
    )


def solution(mesh):
    rows = ("branch", "res")
    return jax.shard_map(
        local,
        mesh=mesh,
        in_specs=(
            P(None, rows, None), P(), P(), P(), P(), P(), P(),
            P(rows, None, None), P(rows, None, None), P(rows), P(rows),
        ),
        out_specs=(P(rows, None, None), P(None, rows, None)),
        check_vma=False,
    )
```

```python
import jax
import jax.numpy as jnp
from jax import lax
from jax.experimental import pallas as pl
from jax.experimental.pallas import tpu as pltpu
from jax.sharding import PartitionSpec as P

MESH = pl.DeviceIdType.MESH
F32 = jnp.float32
BF16 = jnp.bfloat16

SEQS = 64
FEAT = 256
FACTOR = 32
EDGE = 128
LENGTH = 1024
OWN = 8
HALF = 1024
GROUPS = HALF // 128
EPSILON = 1e-05

PARTS = (0, 1, 2)
STEPS = (1, 2, 3)
FORWARD = (0, 1, 3, 2, 3)
DIRECT = (2, 3)
PLANE = tuple((k, m) for k in range(4) for m in range(4) if k or m)


def axes_of(part):
    return (part % 3, (part + 1) % 3, (part + 2) % 3)


def sum_groups(part):
    return pl.ds(3 * part, 3 if part < 2 else GROUPS - 6)


def nt(a, b):
    return lax.dot_general(a, b, (((1,), (1,)), ((), ())), preferred_element_type=F32)


def normalise(x):
    xs = x.astype(F32).reshape(SEQS * OWN, FEAT)
    centred = xs - jnp.mean(xs, axis=-1, keepdims=True)
    rstd = lax.rsqrt(jnp.mean(centred * centred, axis=-1, keepdims=True) + EPSILON)
    return centred * rstd, rstd


def exchange_kernel(
    x_hbm, gain_hbm, w1t_hbm, w2t_hbm, wf_hbm, edge_hbm, cot_hbm, pad_hbm, mol_hbm,
    u_acc, labels, gn_ref, unit_ref, rstd_ref,
    x_ref, gain_ref, w1t_ref, w2t_ref, wf_ref, pad_ref, mol_ref,
    edge, cot, right, left_b, proj, terms, peer_out, peer_in, hop0, hop, slab1, sum1, slab2, sum2, slab3,
    g_acc, gmat, wff, wflat, left_s, grad_s, blk_out, blk_in, fin_s, fin_out, fin_in,
    load_sem,
    ag_send, ag_recv, nb_send, nb_recv, op_send, op_recv, fw_send, fw_recv,
    r0_send, r0_recv, rs_send, rs_recv, pr_send, pr_recv, misc_send, misc_recv,
):
    branch, res = lax.axis_index("branch"), lax.axis_index("res")
    core = res % 2
    first = core == 0
    me = (branch * 2 + res // 32, (res // 8) % 4, (res // 2) % 4)

    def device(at, c):
        return (at[0] // 2, (at[0] % 2) * 32 + at[1] * 8 + at[2] * 2 + c)

    def shifted(axis, k, other=None, m=0):
        at = list(me)
        at[axis] = (at[axis] + k) % 4
        if other is not None:
            at[other] = (at[other] + m) % 4
        return at

    def remote(src, dst, send, recv, to):
        return pltpu.make_async_remote_copy(src, dst, send, recv, device_id=to, device_id_type=MESH)

    sibling = device(me, 1 - core)

    def settle(send, recv, groups, rows, cols):
        block = right.at[0, pl.ds(0, groups), pl.ds(0, rows), pl.ds(0, cols), 0]
        return remote(block, block, send, recv, sibling)

    small = (
        (x_hbm, x_ref), (gain_hbm, gain_ref), (w2t_hbm, w2t_ref), (w1t_hbm, w1t_ref),
        (wf_hbm, wf_ref), (pad_hbm, pad_ref), (mol_hbm, mol_ref),
    )
    small_loads = [
        pltpu.make_async_copy(src, dst, load_sem.at[2 + n]) for n, (src, dst) in enumerate(small)
    ]
    for cp in small_loads:
        cp.start()

    barrier = pltpu.get_barrier_semaphore()
    for part in PARTS:
        axes = axes_of(part)
        for k in STEPS:
            for m in range(4):
                to = device(shifted(axes[0], k, axes[1], m), core)
                pl.semaphore_signal(barrier, inc=1, device_id=to, device_id_type=MESH)
    pl.semaphore_signal(barrier, inc=1, device_id=sibling, device_id_type=MESH)

    cot_loads = [
        pltpu.make_async_copy(cot_hbm.at[i], cot.at[:, :, :, :, pl.ds(i * EDGE, EDGE)], load_sem.at[0])
        for i in range(OWN)
    ]
    edge_load = pltpu.make_async_copy(edge_hbm, edge, load_sem.at[1])
    for cp in cot_loads:
        cp.start()
    edge_load.start()

    for cp in small_loads:
        cp.wait()
    unit, rstd = normalise(x_ref[...])
    unit_ref[...] = unit
    rstd_ref[...] = jnp.broadcast_to(rstd, rstd_ref.shape)
    normed = (unit * gain_ref[...]).astype(BF16)

    lane = lax.broadcasted_iota(jnp.int32, (FACTOR, FEAT), 1)
    row = lax.broadcasted_iota(jnp.int32, (FACTOR, FEAT), 0)
    spread = jnp.where(lane // 8 == row, 1.0, 0.0).astype(BF16)
    w2e = lax.dot_general(
        spread, w2t_ref[...], (((0,), (0,)), ((), ())), preferred_element_type=F32
    ).astype(BF16)

    rows8 = lax.broadcasted_iota(jnp.int32, (OWN, 128), 0)
    keep_col = jnp.zeros((OWN, 128), F32)
    mol_col = jnp.zeros((OWN, 128), F32)
    for i in range(OWN):
        keep_col = jnp.where(rows8 == i, pad_ref[i].astype(F32), keep_col)
        mol_col = jnp.where(rows8 == i, mol_ref[i].astype(F32), mol_col)
    keep_one = keep_col[:, :1]

    lane4 = lax.broadcasted_iota(jnp.int32, (8, OWN, FEAT), 2) % 8
    slot4 = lax.broadcasted_iota(jnp.int32, (8, OWN, FEAT), 0)
    mine = lane4 == slot4
    right_e = nt(normed, w2e).astype(BF16).astype(F32).reshape(8, 8, OWN, FEAT)
    flat = [jnp.sum(jnp.where(mine, right_e[h], 0.0), axis=0) * keep_one for h in range(8)]
    half0 = jnp.concatenate(flat[:4] + [keep_col], axis=1)
    half1 = jnp.concatenate(flat[4:] + [mol_col], axis=1)
    blk_out[...] = jnp.where(first, half1, half0)
    own_blk = jnp.where(first, half0, half1)

    left_s[...] = nt(normed, w1t_ref[...]).astype(BF16).astype(F32)
    wff[...] = wf_ref[...].astype(F32)
    for b in range(FACTOR):
        wflat[:, b * EDGE : (b + 1) * EDGE] = wff[pl.ds(b, FACTOR, stride=FACTOR), :].astype(BF16)
    for i in range(OWN):
        rows = left_s[pl.ds(i, SEQS, stride=OWN), :] * (pad_ref[i].astype(F32) * (1.0 / SEQS))
        left_b[i * SEQS : (i + 1) * SEQS, :] = rows.astype(BF16)

    def proj_steps(start, stop):
        left = left_b[...]

        def step(m, carry):
            for v in range(4):
                n = m * 4 + v
                y = jnp.dot(left, wflat[:, pl.ds(pl.multiple_of(n * 256, 256), 256)], preferred_element_type=F32)
                for i in range(OWN):
                    for h in range(8):
                        tile = y[i * SEQS + h * 8 : i * SEQS + h * 8 + 8]
                        pair = jnp.concatenate([tile[:, :EDGE], tile[:, EDGE:]], axis=0).astype(BF16)
                        top = pl.multiple_of(h * 256 + n * 16, 16)
                        proj[pl.ds(top, 16), i * EDGE : (i + 1) * EDGE] = pair
            return carry

        lax.fori_loop(start, stop, step, 0)

    pl.semaphore_wait(barrier, 37)
    blk_copy = remote(blk_out, blk_in, misc_send.at[0], misc_recv.at[0], sibling)
    blk_copy.start()

    def plane_index(part, phase, at):
        idx = list(at)
        for axis in axes_of(part)[:phase]:
            idx[axis] = slice(None)
        return tuple(idx)

    def block_ref(half, part, phase, at):
        return right.at[(half, pl.ds(3 * part, 3)) + plane_index(part, phase, at)]

    def half_ref(half, part, at, upper):
        idx = list(plane_index(part, 2, at))
        idx[axes_of(part)[0]] = pl.ds(2 * upper, 2)
        return right.at[(half, pl.ds(3 * part, 3)) + tuple(idx)]

    def scattered(part, k, m, receive=False):
        axes = axes_of(part)
        there = shifted(axes[0], (4 - k) % 4, axes[1], (4 - m) % 4)
        block = block_ref(core, part, 0, there if receive else me)
        to = device(there if receive else shifted(axes[0], k, axes[1], m), core)
        return remote(block, block, ag_send.at[part], ag_recv.at[part], to)

    def neighbour(part, k, receive=False):
        axis = axes_of(part)[2]
        at = shifted(axis, 4 - k) if receive else me
        block = block_ref(core, part, 2, at)
        to = device(shifted(axis, 4 - k if receive else k), core)
        return remote(block, block, nb_send.at[part], nb_recv.at[part], to)

    def opposite(part, upper, receive=False):
        axis = axes_of(part)[2]
        k = 3 if upper else 1
        at = shifted(axis, 2) if receive else shifted(axis, 4 - k)
        block = half_ref(core, part, at, upper)
        to = device(shifted(axis, 4 - k if receive else k), core)
        return remote(block, block, op_send.at[part], op_recv.at[part], to)

    def forward(part, k, half):
        if k in (2, 4):
            block = half_ref(half, part, shifted(axes_of(part)[2], 2), int(k == 4))
        else:
            block = block_ref(half, part, 2, shifted(axes_of(part)[2], 4 - k))
        return remote(block, block, fw_send.at[FORWARD[k]], fw_recv.at[FORWARD[k]], sibling)

    def peer_copy(q):
        return remote(peer_out.at[q], peer_in.at[q], pr_send.at[q], pr_recv.at[q], sibling)

    def half_terms(q, half):
        rows = cot[q].reshape(256, OWN * EDGE)
        return nt(rows, proj[pl.ds(pl.multiple_of(half * HALF, HALF), HALF), :])

    def quarter(r):
        return (me[0] + (2, 1, 3, 0)[r]) % 4

    def hop_first(upper):
        groups = sum_groups(0)
        return remote(
            terms.at[groups, quarter(0), pl.ds(2 * upper, 2)], hop0.at[upper, groups],
            r0_send.at[upper], r0_recv.at[upper], device(shifted(0, 3 if upper else 1), core),
        )

    def slab_first(r):
        groups = sum_groups(0)
        return remote(
            terms.at[groups, quarter(r)], slab1.at[r - 1, groups],
            r0_send.at[2], r0_recv.at[2], device(shifted(0, 1 if r == 1 else 3), core),
        )

    def scatter_first(part, r, what):
        groups, q = sum_groups(part), quarter(r)
        up = r % 2 == 0 if what == 0 else what == 1
        there = shifted(part, 2 if what == 0 else (1 if up else 3))
        if part == 1:
            src = terms.at[groups, q, there[1]]
        else:
            src = terms.at[groups, q, :, there[2]]
        dst = hop.at[part - 1, q, groups] if what == 0 else slab1.at[what - 1, groups, q]
        sem = 3 + r if what == 0 else 6 + part
        return remote(
            src, dst, r0_send.at[sem], r0_recv.at[sem],
            device(there if what == 0 and r in DIRECT else shifted(part, 1 if up else 3), core),
        )

    def combine(r):
        q = quarter(r)
        what = 1 if r % 2 == 0 else 2
        settle(r0_send.at[3 + r], r0_recv.at[3 + r], 5, 4, 1).wait_recv()
        for part in (1, 2):
            there = shifted(part, 1 if what == 1 else 3)
            for g in range(3 * part, 3 * part + (3 if part < 2 else GROUPS - 6)):
                idx = (g, q, there[1]) if part == 1 else (g, q, slice(None), there[2])
                terms[idx] = (terms[idx].astype(F32) + hop[part - 1, q, g].astype(F32)).astype(BF16)
            scatter_first(part, r, what).start()

    def peer_half(r):
        q = quarter(r)
        peer_out[q] = half_terms(q, 1 - core).astype(BF16)
        peer_copy(q).start()

    def own_half(r):
        q = quarter(r)
        total = half_terms(q, core)
        peer_copy(q).wait_recv()
        total = (total + peer_in[q].astype(F32)).astype(BF16)
        for g in range(GROUPS):
            terms[g, q] = total[:, g * 128 : (g + 1) * 128].reshape(4, 4, 16, 128)

    def send_terms(r):
        if r == 0:
            for upper in (0, 1):
                hop_first(upper).start()
        for part in (1, 2):
            scatter_first(part, r, 0).start()
            scatter_first(part, r, 2 if r % 2 == 0 else 1).start()
            if r in DIRECT:
                scatter_first(part, r, 1 if r % 2 == 0 else 2).start()

    def combine_first(r):
        upper = r - 1
        hop_first(upper).wait_recv()
        for g in range(3):
            idx = (g, quarter(r), pl.ds(2 * upper, 2))
            terms[idx] = (terms[idx].astype(F32) + hop0[upper, g].astype(F32)).astype(BF16)
        slab_first(r).start()

    proj_steps(0, 2)
    blk_copy.wait_recv()
    theirs = blk_in[...]
    block16 = jnp.concatenate(
        [jnp.where(first, own_blk, theirs), jnp.where(first, theirs, own_blk)], axis=0
    ).astype(BF16)
    for g in range(GROUPS + 1):
        right[core, g, me[0], me[1], me[2]] = block16[:, g * 128 : (g + 1) * 128]
    for k, m in PLANE:
        for part in PARTS:
            scattered(part, k, m).start()

    proj_steps(2, 4)
    pltpu.make_async_copy(cot, cot, load_sem.at[0]).wait()
    peer_half(0)
    peer_half(1)
    peer_half(2)
    own_half(0)
    send_terms(0)
    own_half(1)
    send_terms(1)
    peer_half(3)
    own_half(2)
    send_terms(2)
    for part in PARTS:
        settle(ag_send.at[part], ag_recv.at[part], 5, 3, 3).wait_recv()
    for part in PARTS:
        for k in (1, 3):
            neighbour(part, k).start()
    for part in PARTS:
        forward(part, 0, core).start()
    own_half(3)
    send_terms(3)
    combine_first(1)
    combine(0)
    edge_load.wait()
    for i in range(OWN):
        u_acc[:, :, :, :, i * EDGE : (i + 1) * EDGE] = edge[i].astype(F32)

    def scatter(part, phase, k):
        axes = axes_of(part)
        groups = sum_groups(part)
        to = shifted(axes[phase], k)
        there = to[axes[phase]]
        if phase == 1:
            idx = [slice(None)] * 2
            idx[0 if axes[1] < axes[2] else 1] = there
            src, dst = sum1.at[groups, idx[0], idx[1]], slab2.at[k - 1, groups]
        else:
            src, dst = sum2.at[groups, there], slab3.at[k - 1, groups]
        return remote(
            src, dst, rs_send.at[part, phase - 1], rs_recv.at[part, phase - 1], device(to, core)
        )

    def settled(part, phase):
        send, recv = rs_send.at[part, phase - 1], rs_recv.at[part, phase - 1]
        return settle(send, recv, 9 if part < 2 else 6, 4 if phase == 1 else 1, 1)

    def scatter_add(part, phase):
        axes = axes_of(part)
        here = me[axes[phase]]
        first_group, count = 3 * part, 3 if part < 2 else GROUPS - 6
        if phase == 0:
            sem, tiles = ((2, (6, 4, 4)), (7, (6, 4, 4)), (8, (4, 4, 4)))[part]
            settle(r0_send.at[sem], r0_recv.at[sem], *tiles).wait_recv()
        else:
            settled(part, phase).wait_recv()
        for g in range(first_group, first_group + count):
            if phase == 0 and part > 0:
                for r in DIRECT:
                    q = quarter(r)
                    late = slab1[0, g, q].astype(F32) + hop[part - 1, q, g].astype(F32)
                    slab1[0, g, q] = late.astype(BF16)
            if phase == 0:
                idx = [slice(None)] * 3
                idx[axes[0]] = here
                total = terms[g, idx[0], idx[1], idx[2]].astype(F32)
                for k in range(2):
                    total += slab1[k, g].astype(F32)
                sum1[g] = total.astype(BF16)
            elif phase == 1:
                idx = [slice(None)] * 2
                idx[0 if axes[1] < axes[2] else 1] = here
                total = sum1[g, idx[0], idx[1]].astype(F32)
                for k in range(3):
                    total += slab2[k, g].astype(F32)
                sum2[g] = total.astype(BF16)
            else:
                total = sum2[g, here].astype(F32)
                for k in range(3):
                    total += slab3[k, g].astype(F32)
                fin_s[:, g * 128 : (g + 1) * 128] = total
        if phase < 2:
            for k in STEPS:
                scatter(part, phase + 1, k).start()

    def flat_plane(ref, lead, part, k):
        idx = plane_index(part, 2, shifted(axes_of(part)[2], (4 - k) % 4))
        return ref[lead + idx].reshape(256, ref.shape[-1])

    def count_of(part):
        return 3 if part < 2 else GROUPS - 6

    def left_plane(half, part, k):
        count = count_of(part)
        block = jnp.concatenate(
            [flat_plane(right, (half, 3 * part + n), part, k) for n in range(count)], axis=1
        )
        prod = lax.dot_general(
            block, flat_plane(cot, (), part, k), (((0,), (0,)), ((), ())), preferred_element_type=F32
        )
        rows = pl.ds(pl.multiple_of(half * HALF + part * 384, 128), count * 128)
        if k == 0:
            g_acc[rows, :] = prod
            return
        prod = prod + g_acc[rows, :]
        if k != 2:
            g_acc[rows, :] = prod
            return
        for n in range(count):
            gi = 3 * part + n
            for b in range(16):
                tile = prod[n * 128 + b * 8 : n * 128 + b * 8 + 8]
                lo = ((gi % 2) * 16 + b) * EDGE
                for m in range(OWN // 2):
                    pair = jnp.concatenate(
                        [tile[:, m * 256 : m * 256 + EDGE], tile[:, m * 256 + EDGE : m * 256 + 256]], axis=0
                    ).astype(BF16)
                    top = pl.multiple_of((half * 4 + gi // 2) * 64 + m * 16, 16)
                    gmat[pl.ds(top, 16), lo : lo + EDGE] = pair

    def pair_plane(part, k):
        count = count_of(part)
        lhs = jnp.concatenate(
            [flat_plane(right, (half, 3 * part + n), part, k) for half in range(2) for n in range(count)], axis=1
        )
        rhs = jnp.concatenate(
            [proj[half * HALF + part * 384 : half * HALF + part * 384 + count * 128, :] for half in range(2)], axis=0
        )
        u = jnp.dot(lhs, rhs, preferred_element_type=F32)
        idx = plane_index(part, 2, shifted(axes_of(part)[2], (4 - k) % 4))
        u_acc[idx] = u_acc[idx] + u.reshape(4, 4, 16, OWN * EDGE)

    def forwarded(k):
        settle(fw_send.at[FORWARD[k]], fw_recv.at[FORWARD[k]], 9, 4, 4).wait_recv()

    def left_own(k):
        for part in PARTS:
            left_plane(core, part, k)

    def left_other(k):
        for part in PARTS:
            left_plane(1 - core, part, k)

    def pair(k):
        for part in PARTS:
            pair_plane(part, k)

    def neighbours():
        for part in PARTS:
            settle(nb_send.at[part], nb_recv.at[part], 6, 4, 4).wait_recv()
            for k in (1, 3):
                opposite(part, int(k == 3)).start()
        for k in (1, 3):
            for part in PARTS:
                forward(part, k, core).start()

    def opposites():
        for part in PARTS:
            settle(op_send.at[part], op_recv.at[part], 3, 4, 4).wait_recv()
            for upper in (0, 1):
                forward(part, 2 + 2 * upper, core).start()

    def reduce(phase):
        if phase == 0:
            for r in DIRECT:
                settle(r0_send.at[3 + r], r0_recv.at[3 + r], 5, 4, 1).wait_recv()
        for part in PARTS:
            scatter_add(part, phase)

    def left_gradient():
        gl = nt(gmat[...], wflat[...])
        for h in range(8):
            for i in range(OWN):
                tile = gl[h * 64 + i * 8 : h * 64 + i * 8 + 8] * (pad_ref[i].astype(F32) * (1.0 / SEQS))
                grad_s[pl.ds(h * 64 + i, 8, stride=OWN), :] = tile
        gn_ref[...] = jnp.dot(grad_s[...].astype(BF16), w1t_ref[...], preferred_element_type=F32)

    left_own(0)
    combine(1)
    combine_first(2)
    forwarded(0)
    left_other(0)
    pair(0)
    neighbours()
    left_own(1)
    left_own(3)
    forwarded(1)
    left_other(1)
    reduce(0)
    forwarded(3)
    left_other(3)
    opposites()
    pair(1)
    left_own(2)
    reduce(1)
    pair(3)
    forwarded(2)
    left_other(2)
    pair(2)
    for half in range(2):
        labels[half] = right[half, GROUPS]
    reduce(2)
    fin = fin_s[...]
    fin_out[...] = jnp.where(first, fin[8:], fin[:8])
    fin_mine = jnp.where(first, fin[:8], fin[8:])
    fin_copy = remote(fin_out, fin_in, misc_send.at[1], misc_recv.at[1], sibling)
    fin_copy.start()
    left_gradient()

    fin_copy.wait_recv()
    fin_theirs = fin_in[...]
    lo_half = jnp.where(first, fin_mine, fin_theirs) * keep_one
    hi_half = jnp.where(first, fin_theirs, fin_mine) * keep_one
    spread_rows = []
    for h in range(8):
        src = lo_half if h < 4 else hi_half
        base = src[:, (h % 4) * 256 : (h % 4) * 256 + 256]
        spread_rows.append(jnp.where(mine, base[None], 0.0).reshape(8 * OWN, FEAT))
    gr = jnp.concatenate(spread_rows, axis=0).astype(BF16)
    gn_ref[...] += jnp.dot(gr, w2e, preferred_element_type=F32)

    blk_copy.wait_send()
    fin_copy.wait_send()
    for part in PARTS:
        for phase in (1, 2):
            settled(part, phase).wait_send()
        settle(ag_send.at[part], ag_recv.at[part], 5, 3, 3).wait_send()
        settle(nb_send.at[part], nb_recv.at[part], 6, 4, 4).wait_send()
        settle(op_send.at[part], op_recv.at[part], 3, 4, 4).wait_send()
    for k in range(4):
        settle(fw_send.at[k], fw_recv.at[k], 9, 4, 4).wait_send()
    for r in range(4):
        settle(r0_send.at[3 + r], r0_recv.at[3 + r], 5, 4, 1).wait_send()
        peer_copy(r).wait_send()
    for sem, tiles in ((2, (6, 4, 4)), (7, (6, 4, 4)), (8, (4, 4, 4))):
        settle(r0_send.at[sem], r0_recv.at[sem], *tiles).wait_send()
    for upper in (0, 1):
        hop_first(upper).wait_send()


def finish_kernel(
    u_ref, labels, gn_ref, unit_ref, rstd_ref, gain_ref, off_ref, smo_ref, pad_ref, mol_ref,
    pair_out, grad_out, held, grad, sems,
):
    def store(q):
        rows = pl.ds(q * 128, 128)
        return pltpu.make_async_copy(held.at[:, rows], pair_out.at[:, rows], sems.at[q])

    grad_store = pltpu.make_async_copy(grad, grad_out, sems.at[8])

    def pair(q):
        for lo in range(q * 128, q * 128 + 128, 64):
            rows = slice(lo, lo + 64)
            keep_j = labels[0, rows, :].astype(F32)
            mol_j = labels[1, rows, :].astype(F32)
            apart = keep_j * off_ref[...]
            together = keep_j * (off_ref[...] + smo_ref[...])
            for i in range(OWN):
                extra = jnp.where(mol_j == mol_ref[i].astype(F32), together, apart) * pad_ref[i].astype(F32)
                held[i, rows, :] = (u_ref[rows, i * EDGE : (i + 1) * EDGE] + extra).astype(BF16)
        store(q).start()

    for q in range(4):
        pair(q)
    unit = unit_ref[...]
    gained = gn_ref[...] * gain_ref[...]
    result = rstd_ref[:, :1] * (
        gained
        - jnp.mean(gained, axis=-1, keepdims=True)
        - unit * jnp.mean(gained * unit, axis=-1, keepdims=True)
    )
    grad[...] = result.reshape(SEQS, OWN, FEAT)
    grad_store.start()
    for q in range(4, 8):
        pair(q)
    for q in range(8):
        store(q).wait()
    grad_store.wait()


def local(x, gain, w1, w2, wf, off, smo, edge, cot, pad, mol):
    vmem = pl.BlockSpec(memory_space=pltpu.VMEM)
    smem = pl.BlockSpec(memory_space=pltpu.SMEM)
    hbm = pl.BlockSpec(memory_space=pl.ANY)
    dma = pltpu.SemaphoreType.DMA
    gain = gain.reshape(1, FEAT)
    operands = (x, gain, w1.T, w2.T, wf) + tuple(
        v.reshape(OWN, 4, 4, 4, 16, EDGE) for v in (edge, cot)
    ) + (pad, mol)
    u, labels, gn, unit, rstd = pl.pallas_call(
        exchange_kernel,
        out_shape=(
            pltpu.VMEM((4, 4, 4, 16, OWN * EDGE), F32),
            pltpu.VMEM((2, 4, 4, 4, 16, 128), BF16),
            pltpu.VMEM((SEQS * OWN, FEAT), F32),
            pltpu.VMEM((SEQS * OWN, FEAT), F32),
            pltpu.VMEM((SEQS * OWN, 128), F32),
        ),
        in_specs=[hbm] * 9,
        out_specs=(vmem,) * 5,
        scratch_shapes=[
            pltpu.VMEM((SEQS, OWN, FEAT), BF16),
            pltpu.VMEM((1, FEAT), F32),
            pltpu.VMEM((FACTOR, FEAT), BF16),
            pltpu.VMEM((FACTOR, FEAT), BF16),
            pltpu.VMEM((FACTOR * FACTOR, EDGE), BF16),
            pltpu.SMEM((OWN,), jnp.int32),
            pltpu.SMEM((OWN,), jnp.int32),
            pltpu.VMEM((OWN, 4, 4, 4, 16, EDGE), BF16),
            pltpu.VMEM((4, 4, 4, 16, OWN * EDGE), BF16),
            pltpu.VMEM((2, GROUPS + 1, 4, 4, 4, 16, 128), BF16),
            pltpu.VMEM((SEQS * OWN, FACTOR), BF16),
            pltpu.VMEM((2 * HALF, OWN * EDGE), BF16),
            pltpu.VMEM((GROUPS, 4, 4, 4, 16, 128), BF16),
            pltpu.VMEM((4, 256, HALF), BF16),
            pltpu.VMEM((4, 256, HALF), BF16),
            pltpu.VMEM((2, 3, 2, 4, 16, 128), BF16),
            pltpu.VMEM((2, 4, GROUPS, 4, 16, 128), BF16),
            pltpu.VMEM((2, GROUPS, 4, 4, 16, 128), BF16),
            pltpu.VMEM((GROUPS, 4, 4, 16, 128), BF16),
            pltpu.VMEM((3, GROUPS, 4, 16, 128), BF16),
            pltpu.VMEM((GROUPS, 4, 16, 128), BF16),
            pltpu.VMEM((3, GROUPS, 16, 128), BF16),
            pltpu.VMEM((2 * HALF, OWN * EDGE), F32),
            pltpu.VMEM((SEQS * OWN, FACTOR * EDGE), BF16),
            pltpu.VMEM((FACTOR * FACTOR, EDGE), F32),
            pltpu.VMEM((FACTOR, FACTOR * EDGE), BF16),
            pltpu.VMEM((SEQS * OWN, FACTOR), F32),
            pltpu.VMEM((SEQS * OWN, FACTOR), F32),
            pltpu.VMEM((OWN, HALF + 128), F32),
            pltpu.VMEM((OWN, HALF + 128), F32),
            pltpu.VMEM((16, HALF), F32),
            pltpu.VMEM((OWN, HALF), F32),
            pltpu.VMEM((OWN, HALF), F32),
            dma((9,)),
            dma((3,)),
            dma((3,)),
            dma((3,)),
            dma((3,)),
            dma((3,)),
            dma((3,)),
            dma((4,)),
            dma((4,)),
            dma((9,)),
            dma((9,)),
            dma((3, 2)),
            dma((3, 2)),
            dma((4,)),
            dma((4,)),
            dma((2,)),
            dma((2,)),
        ],
        compiler_params=pltpu.CompilerParams(
            collective_id=0, has_side_effects=True, vmem_limit_bytes=50 * 2**20
        ),
        name="outer_product_mean",
    )(*(pltpu.with_memory_space_constraint(v, pltpu.HBM) for v in operands))
    return pl.pallas_call(
        finish_kernel,
        out_shape=(
            jax.ShapeDtypeStruct(edge.shape, BF16),
            jax.ShapeDtypeStruct(x.shape, F32),
        ),
        in_specs=[vmem] * 8 + [smem, smem],
        out_specs=(hbm, hbm),
        scratch_shapes=[
            pltpu.VMEM((OWN, LENGTH, EDGE), BF16),
            pltpu.VMEM((SEQS, OWN, FEAT), F32),
            dma((9,)),
        ],
        compiler_params=pltpu.CompilerParams(vmem_limit_bytes=16 * 2**20),
        name="finish",
    )(
        u.reshape(LENGTH, OWN * EDGE), labels.reshape(2, LENGTH, 128), gn, unit, rstd, gain,
        off.reshape(1, EDGE), smo.reshape(1, EDGE), pad, mol,
    )


def solution(mesh):
    rows = ("branch", "res")
    return jax.shard_map(
        local,
        mesh=mesh,
        in_specs=(
            P(None, rows, None), P(), P(), P(), P(), P(), P(),
            P(rows, None, None), P(rows, None, None), P(rows), P(rows),
        ),
        out_specs=(P(rows, None, None), P(None, rows, None)),
        check_vma=False,
    )
```
